128 devices in a mesh: dap: 64 (over z, y, x_hi, core), ch: 2 (over x_lo).
Axes of the slice: x: 4 (x_hi: 2, x_lo: 2; x = x_hi * 2 + x_lo), y: 4, z: 4, core: 2. Of those that a mesh axis runs over, the one named last changes fastest.
Arguments:
- pair: bfloat16 [256, 256, 128], P('dap'), may hold values from -6 to 6
- chain_lengths: int32 [4], replicated, may hold values from 32 to 64
- ln_gain: float32 [128], replicated, may hold values from 0.25 to 1.75
- ln_bias: float32 [128], replicated, may hold values from -3 to 3
- proj_weight: bfloat16 [4, 128, 128], P(None, None, 'ch'), may hold values from -0.5 to 0.5
- proj_bias: float32 [4, 128], P(None, 'ch'), may hold values from -3 to 3
- out_gain: float32 [128], P('ch'), may hold values from 0.25 to 1.75
- out_bias: float32 [128], P('ch'), may hold values from -3 to 3
- w_out: bfloat16 [128, 128], P('ch'), may hold values from -0.5 to 0.5
- out_shift: float32 [128], replicated, may hold values from -3 to 3
- w_gate: bfloat16 [128, 128], replicated, may hold values from -0.5 to 0.5
- gate_bias: float32 [128], replicated, may hold values from -3 to 3
- cotangent: bfloat16 [256, 256, 128], P('dap', 'ch'), may hold values from -6 to 6
Outputs:
- update: bfloat16 [256, 256, 128], P('dap', 'ch')
- pair_grad: bfloat16 [256, 256, 128], P('dap', 'ch')
The draws below stay inside these ranges and needn't reach their ends.
Inputs may be any that keep to these rules, and one draw needn't show every extreme that they name: Chain m occupies residues m * 64 to (m + 1) * 64 - 1, of which the first chain_lengths[m] are real and the rest are padding.
All inputs are finite; a program needn't handle non-finite values.
Results may differ from the reference program's by a relative error of at most 0.012.
Values may be sent and summed in bfloat16 or wider, within the bound.
A program may use at most 64 MiB of HBM per device.

```python
import jax
import jax.numpy as jnp
from jax import lax

C = 128
HID = 128
CHAINS = 4
N = 256
SLOT = 64


def plant(array, stream_key, smallest, top_value):
    longest = array.shape.index(max(array.shape))
    spots = []
    for shift in (0, 1):
        where = [jax.random.randint(jax.random.fold_in(stream_key, axis), (), 0, length) for axis, length in enumerate(array.shape)]
        where[longest] = (where[longest] + shift) % array.shape[longest]
        spots.append(tuple(where))
    return array.at[spots[0]].set(smallest).at[spots[1]].set(top_value)


def shard_levels(stream_key, dims, shards, smallest, top_value):
    def one(dim, parts):
        draws = jax.random.uniform(jax.random.fold_in(jax.random.fold_in(stream_key, 6), dim), (parts,), jnp.float32, smallest / len(shards), top_value / len(shards))
        return jnp.repeat(jnp.exp(draws), dims[dim] // parts).reshape((-1,) + (1,) * (len(dims) - dim - 1))

    gain = one(*shards[0])
    for cut in shards[1:]:
        gain = gain * one(*cut)
    return gain


def gaussian(key, shape, deviation, most, cuts=(), kind=jnp.bfloat16):
    result = deviation * jax.random.normal(key, shape, jnp.float32)
    if cuts:
        result = result * shard_levels(key, shape, cuts, -0.22, 0.18)
    return jnp.clip(result, -most, most).astype(kind)


def setup_inputs(seed: int = 0) -> dict:
    arg_keys = jax.random.split(jax.random.key(seed), 14)
    pair = gaussian(arg_keys[0], (N, N, C), 1.0, 6.0, ((0, 64),))
    chain_lengths = plant(jax.random.randint(arg_keys[1], (CHAINS,), SLOT // 2, SLOT + 1), jax.random.fold_in(arg_keys[1], 1), SLOT // 2, SLOT).astype(jnp.int32)
    ln_gain = jnp.clip(1.0 + 0.15 * jax.random.normal(arg_keys[2], (C,), jnp.float32), 0.25, 1.75)
    ln_bias = gaussian(arg_keys[3], (C,), 0.5, 3.0, (), jnp.float32)
    proj_weight = gaussian(arg_keys[4], (4, C, HID), C ** -0.5, 0.5, ((2, 2),))
    proj_bias = gaussian(arg_keys[5], (4, HID), 0.5, 3.0, ((1, 2),), jnp.float32)
    out_gain = jnp.clip(1.0 + 0.15 * jax.random.normal(arg_keys[6], (HID,), jnp.float32), 0.25, 1.75)
    out_bias = gaussian(arg_keys[7], (HID,), 0.5, 3.0, ((0, 2),), jnp.float32)
    w_out = gaussian(arg_keys[8], (HID, C), HID ** -0.5, 0.5, ((0, 2),))
    out_shift = gaussian(arg_keys[9], (C,), 0.5, 3.0, (), jnp.float32)
    w_gate = gaussian(arg_keys[10], (C, C), C ** -0.5, 0.5)
    gate_bias = gaussian(arg_keys[11], (C,), 0.5, 3.0, (), jnp.float32)
    cotangent = gaussian(arg_keys[12], (N, N, C), 1.0, 6.0, ((0, 64), (1, 2)))
    return {"pair": pair, "chain_lengths": chain_lengths, "ln_gain": ln_gain, "ln_bias": ln_bias, "proj_weight": proj_weight, "proj_bias": proj_bias, "out_gain": out_gain, "out_bias": out_bias, "w_out": w_out, "out_shift": out_shift, "w_gate": w_gate, "gate_bias": gate_bias, "cotangent": cotangent}


epsilon = 1e-05

def layer_stats(values):
    mean = lax.optimization_barrier(jnp.mean(values, axis=-1, keepdims=True))
    square = lax.optimization_barrier(jnp.mean(values * values, axis=-1, keepdims=True))
    return (mean, lax.rsqrt(square - mean * mean + epsilon))

def reference(pair, chain_lengths, ln_gain, ln_bias, proj_weight, proj_bias, out_gain, out_bias, w_out, out_shift, w_gate, gate_bias, cotangent):
    residues = pair.shape[0]
    slot_size = residues // CHAINS
    position = jnp.arange(residues, dtype=jnp.int32)
    chain_limit = chain_lengths[(position // slot_size).astype(jnp.int32)]
    present = (position % slot_size < chain_limit).astype(jnp.float32)
    pair_mask = (present[:, None] * present[None, :])[:, :, None]
    pair_float = pair.astype(jnp.float32)
    pair_mean, pair_scale = layer_stats(pair_float)
    pair_norm = (pair_float - pair_mean) * pair_scale
    normed = (pair_norm * ln_gain + ln_bias).astype(jnp.bfloat16)
    flattened = normed.reshape(residues * residues, C)
    projected = []
    for member in range(4):
        value = jnp.dot(flattened, proj_weight[member], preferred_element_type=jnp.float32) + proj_bias[member]
        projected.append(value.reshape(residues, residues, HID))
    gate_left = jax.nn.sigmoid(projected[0])
    gate_right = jax.nn.sigmoid(projected[2])
    left_edge = (gate_left * projected[1] * pair_mask).astype(jnp.bfloat16)
    right_edge = (gate_right * projected[3] * pair_mask).astype(jnp.bfloat16)
    left_float = left_edge.astype(jnp.float32)
    right_float = right_edge.astype(jnp.float32)
    triangle = jnp.einsum('ikc,jkc->ijc', left_float, right_float, precision=lax.Precision.HIGHEST)
    tri_mean, tri_scale = layer_stats(triangle)
    tri_norm = (triangle - tri_mean) * tri_scale
    tri_out = (tri_norm * out_gain + out_bias).astype(jnp.bfloat16)
    output_sum = jnp.dot(tri_out.reshape(-1, HID), w_out, preferred_element_type=jnp.float32).reshape(residues, residues, C) + out_shift
    gate_value = jax.nn.sigmoid(jnp.dot(flattened, w_gate, preferred_element_type=jnp.float32).reshape(residues, residues, C) + gate_bias)
    update = (gate_value * output_sum).astype(jnp.bfloat16)
    cot_float = cotangent.astype(jnp.float32)
    grad_out = (cot_float * gate_value).astype(jnp.bfloat16)
    grad_gate = (cot_float * output_sum * gate_value * (1.0 - gate_value)).astype(jnp.bfloat16)
    grad_normed = jnp.dot(grad_out.reshape(-1, C), w_out.T, preferred_element_type=jnp.float32).reshape(residues, residues, HID)
    grad_scaled = grad_normed * out_gain
    grad_tri = (tri_scale * (grad_scaled - lax.optimization_barrier(jnp.mean(grad_scaled, axis=-1, keepdims=True)) - tri_norm * lax.optimization_barrier(jnp.mean(grad_scaled * tri_norm, axis=-1, keepdims=True)))).astype(jnp.bfloat16)
    tri_float = grad_tri.astype(jnp.float32)
    grad_left = jnp.einsum('ijc,jkc->ikc', tri_float, right_float, precision=lax.Precision.HIGHEST)
    grad_right = jnp.einsum('ijc,ikc->jkc', tri_float, left_float, precision=lax.Precision.HIGHEST)
    grad_proj = [(grad_left * projected[1] * pair_mask * gate_left * (1.0 - gate_left)).astype(jnp.bfloat16), (grad_left * gate_left * pair_mask).astype(jnp.bfloat16), (grad_right * projected[3] * pair_mask * gate_right * (1.0 - gate_right)).astype(jnp.bfloat16), (grad_right * gate_right * pair_mask).astype(jnp.bfloat16)]
    grad_pair = jnp.dot(grad_gate.reshape(-1, C), w_gate.T, preferred_element_type=jnp.float32)
    for member in range(4):
        grad_pair = grad_pair + jnp.dot(grad_proj[member].reshape(-1, HID), proj_weight[member].T, preferred_element_type=jnp.float32)
    pair_scaled = grad_pair.reshape(residues, residues, C) * ln_gain
    pair_grad = (pair_scale * (pair_scaled - lax.optimization_barrier(jnp.mean(pair_scaled, axis=-1, keepdims=True)) - pair_norm * lax.optimization_barrier(jnp.mean(pair_scaled * pair_norm, axis=-1, keepdims=True)))).astype(jnp.bfloat16)
    return (update, pair_grad)
```

```python
import jax
import jax.numpy as jnp
from jax import lax
from jax.experimental import pallas as pl
from jax.experimental.pallas import tpu as pltpu
from jax.sharding import PartitionSpec as P

EPS = 1e-05
F32 = jnp.float32
BF16 = jnp.bfloat16
MESH = pl.DeviceIdType.MESH


def sigmoid(x):
    return 0.5 * jnp.tanh(0.5 * x) + 0.5


def mm(a, b):
    return lax.dot_general(a, b, (((1,), (0,)), ((), ())), preferred_element_type=F32)


def mm_nt(a, b):
    return lax.dot_general(a, b, (((1,), (1,)), ((), ())), preferred_element_type=F32)


def mm_tn(a, b):
    return lax.dot_general(a, b, (((0,), (0,)), ((), ())), preferred_element_type=F32)


def column(block, n, rows):
    return jnp.broadcast_to(block[0:rows, n : n + 1], (rows, 128))


def mean0(x):
    return jnp.sum(x, axis=0, keepdims=True) * (1.0 / 128.0)


def kernel(
    pair,
    lens,
    ln_gain,
    ln_bias,
    pw,
    pb,
    out_gain,
    out_bias,
    w_out,
    out_shift,
    w_gate,
    gate_bias,
    cot,
    update,
    pair_grad,
    wt,
    wo,
    hv,
    vec,
    pnorm,
    pscale,
    normed,
    s1f,
    s1,
    r1,
    r1f,
    lmat,
    rmat,
    s2,
    r2,
    s3,
    r3,
    gmat,
    s4f,
    s4,
    r4,
    r4f,
    factor,
    gate_t,
    cot_t,
    gs_t,
    m1_t,
    tn_t,
    part_t,
    wo_t,
    back_w,
    gp,
    wsem_s,
    wsem_r,
    ssem,
    rsem,
):
    p = lax.axis_index("dap")
    g = lax.axis_index("ch")
    me = g * 64 + p

    barrier = pltpu.get_barrier_semaphore()

    def greet(k, carry):
        t = lax.rem(me + k, 128)
        pl.semaphore_signal(
            barrier, inc=1, device_id=(lax.rem(t, 64), t // 64), device_id_type=MESH
        )
        return carry

    lax.fori_loop(1, 128, greet, 0)

    for m in range(4):
        wt[g, m * 64 : (m + 1) * 64, :] = pw[m].T
    wo[g] = w_out[...]
    hv[g] = jnp.zeros((8, 128), F32)
    hv[g, 0:4, 0:64] = pb[...]
    hv[g, 4:5, 0:64] = out_gain[...]
    hv[g, 5:6, 0:64] = out_bias[...]
    vec[...] = jnp.zeros((8, 128), F32)
    vec[0:1, :] = ln_gain[...]
    vec[1:2, :] = ln_bias[...]
    vec[2:3, :] = out_shift[...]
    vec[3:4, :] = gate_bias[...]
    vcol = vec[...].T
    gain_c = column(vcol, 0, 128)
    bias_c = column(vcol, 1, 128)
    hcol = hv[g].T
    proj_c = [column(hcol, m, 64) for m in range(4)]

    lane = lax.broadcasted_iota(jnp.int32, (1, 128), 1)
    low = lane < 64
    slot = jnp.where(low, lane, lane - 64)

    def present_columns(first_chain):
        limit = jnp.where(low, lens[first_chain], lens[first_chain + 1])
        return jnp.where(slot < limit, 1.0, 0.0)

    row_limit = jnp.full((1, 128), lens[p // 16], jnp.int32)
    row_present = [
        jnp.where(row_limit > lax.rem(p * 4 + i, 64), 1.0, 0.0) for i in range(4)
    ]

    columns = [present_columns(0), present_columns(2)]
    for i in range(4):
        for kh in range(2):
            t = i * 2 + kh
            x = pair[i, kh * 128 : (kh + 1) * 128, :].T.astype(F32)
            mean = mean0(x)
            scale = lax.rsqrt(mean0(x * x) - mean * mean + EPS)
            norm = (x - mean) * scale
            pnorm[t] = norm
            pscale[t] = scale
            nb = (norm * gain_c + bias_c).astype(BF16)
            normed[t] = nb
            mask = row_present[i] * columns[kh]
            pr = mm(wt[g], nb)
            left = sigmoid(pr[0:64] + proj_c[0]) * (pr[64:128] + proj_c[1]) * mask
            right = sigmoid(pr[128:192] + proj_c[2]) * (pr[192:256] + proj_c[3]) * mask
            s1f[pl.ds(i * 4 + kh, 64, stride=16), :] = left
            s1f[pl.ds(i * 4 + 2 + kh, 64, stride=16), :] = right
    s1[...] = s1f[...].reshape(64, 16, 128).astype(BF16)

    pl.semaphore_wait(barrier, 127)

    own1 = pltpu.make_async_copy(s1.at[p], r1.at[p], rsem.at[0])
    own1.start()

    def send1(k, carry):
        t = lax.rem(p + k, 64)
        pltpu.make_async_remote_copy(
            src_ref=s1.at[t],
            dst_ref=r1.at[p],
            send_sem=ssem.at[0],
            recv_sem=rsem.at[0],
            device_id=(t, g),
            device_id_type=MESH,
        ).start()
        return carry

    lax.fori_loop(1, 64, send1, 0)

    swaps = [
        pltpu.make_async_remote_copy(
            src_ref=ref.at[g],
            dst_ref=ref.at[g],
            send_sem=wsem_s.at[n],
            recv_sem=wsem_r.at[n],
            device_id=(p, 1 - g),
            device_id_type=MESH,
        )
        for n, ref in enumerate((wt, wo, hv))
    ]
    for swap in swaps:
        swap.start()

    gate_w = w_gate[...].T
    gate_c = column(vcol, 3, 128)
    own_columns = present_columns(g * 2)
    for i in range(4):
        gate = sigmoid(mm(gate_w, normed[i * 2 + g]) + gate_c)
        gate_t[i] = gate
        cot_t[i] = cot[i].T.astype(F32)
    for swap in swaps:
        swap.wait()
    halves = [hv[0].T, hv[1].T]
    full = [
        jnp.concatenate([column(halves[0], n, 64), column(halves[1], n, 64)], axis=0)
        for n in (4, 5)
    ]
    wo_full = wo[...].reshape(128, 128)
    for i in range(4):
        grad_out = (cot_t[i] * gate_t[i]).astype(BF16)
        gs = mm(wo_full, grad_out) * full[0]
        gs_t[i] = gs
        m1_t[i] = mean0(gs)
    wo_t[...] = wo_full.T
    back_w[...] = wt[...].reshape(512, 128).astype(F32).T.astype(BF16)

    for h in range(2):
        bias = [column(halves[h], m, 64) for m in range(4)]
        rows = slice(h * 64, (h + 1) * 64)
        for i in range(4):
            pr = mm(wt[h], normed[i * 2 + g])
            mask = row_present[i] * own_columns
            for side in range(2):
                n = side * 2
                s = sigmoid(pr[n * 64 : n * 64 + 64] + bias[n])
                sm = s * mask
                value = pr[n * 64 + 64 : n * 64 + 128] + bias[n + 1]
                factor[i, n, rows, :] = value * sm * (1.0 - s)
                factor[i, n + 1, rows, :] = sm

    pltpu.make_async_copy(r1, r1, rsem.at[0]).wait()
    r1f[...] = r1[...].reshape(1024, 128).astype(F32)
    for kh in range(2):
        cols = slice(kh * 128, (kh + 1) * 128)
        lmat[:, cols] = r1f[pl.ds(kh, 256, stride=4), :].astype(BF16)
        rmat[:, cols] = r1f[pl.ds(2 + kh, 256, stride=4), :].astype(BF16)
    for h in range(2):
        s2[h * 256 : (h + 1) * 256, :] = mm_nt(
            lmat[...], rmat[h * 128 : (h + 1) * 128, :]
        )

    def spread(source, target, n):
        mine = pl.ds(pl.multiple_of(me * 4, 4), 4)
        pltpu.make_async_copy(source.at[mine], target.at[mine], rsem.at[n]).start()

        def send(k, carry):
            t = lax.rem(me + k, 128)
            pltpu.make_async_remote_copy(
                src_ref=source.at[pl.ds(pl.multiple_of(t * 4, 4), 4)],
                dst_ref=target.at[mine],
                send_sem=ssem.at[n],
                recv_sem=rsem.at[n],
                device_id=(lax.rem(t, 64), t // 64),
                device_id_type=MESH,
            ).start()
            return carry

        lax.fori_loop(1, 128, send, 0)

    spread(s2, r2, 1)
    pltpu.make_async_copy(r2, r2, rsem.at[1]).wait()

    for i in range(4):
        tri = r2[pl.ds(i, 128, stride=4), :]
        mean = mean0(tri)
        scale = lax.rsqrt(mean0(tri * tri) - mean * mean + EPS)
        tn = (tri - mean) * scale
        tn_t[i] = tn
        gs = gs_t[i]
        grad = scale * (gs - m1_t[i] - tn * mean0(gs * tn))
        s3[pl.ds(i, 128, stride=4), :] = grad
    spread(s3, r3, 2)

    shift_c = column(vcol, 2, 128)
    for i in range(4):
        tri_out = (tn_t[i] * full[0] + full[1]).astype(BF16)
        out_sum = mm(wo_t[...], tri_out) + shift_c
        gate = gate_t[i]
        gated = gate * out_sum
        update[i] = gated.T.astype(BF16)
        grad_gate = (cot_t[i] * gated * (1.0 - gate)).astype(BF16)
        part_t[i] = mm(w_gate[...], grad_gate)

    pltpu.make_async_copy(r3, r3, rsem.at[2]).wait()
    for h in range(2):
        gmat[:, h * 128 : (h + 1) * 128] = r3[h * 256 : (h + 1) * 256, :].astype(BF16)
    grads = (mm(gmat[...], rmat[...]), mm_tn(gmat[...], lmat[...]))
    for side in range(2):
        for h in range(2):
            s4f[pl.ds(h * 512 + side, 256, stride=2), :] = grads[side][
                :, h * 128 : (h + 1) * 128
            ]
    s4[...] = s4f[...].reshape(128, 8, 128).astype(BF16)
    pltpu.make_async_copy(s4.at[me], r4.at[me], rsem.at[3]).start()

    def send4(k, carry):
        t = lax.rem(me + k, 128)
        pltpu.make_async_remote_copy(
            src_ref=s4.at[t],
            dst_ref=r4.at[me],
            send_sem=ssem.at[3],
            recv_sem=rsem.at[3],
            device_id=(lax.rem(t, 64), t // 64),
            device_id_type=MESH,
        ).start()
        return carry

    lax.fori_loop(1, 128, send4, 0)
    pltpu.make_async_copy(r4, r4, rsem.at[3]).wait()

    r4f[...] = r4[...].astype(F32).reshape(1024, 128)
    for i in range(4):
        for side in range(2):
            edge = r4f[pl.ds(i * 2 + side, 128, stride=8), :]
            for n in range(2):
                m = side * 2 + n
                prod = (edge * factor[i, m]).astype(BF16)
                for h in range(2):
                    at = h * 256 + m * 64
                    gp[at : at + 64, i * 128 : (i + 1) * 128] = prod[
                        h * 64 : (h + 1) * 64
                    ]
    for i in range(4):
        grad = mm(back_w[...], gp[:, i * 128 : (i + 1) * 128]) + part_t[i]
        ps = grad * gain_c
        norm = pnorm[i * 2 + g]
        own = pscale[i * 2 + g] * (ps - mean0(ps) - norm * mean0(ps * norm))
        pair_grad[i] = own.T.astype(BF16)

    blocks = s1.at[pl.ds(0, 63)]
    pltpu.make_async_copy(blocks, blocks, ssem.at[0]).wait()
    for n, ref in ((1, s2), (2, s3)):
        blocks = ref.at[pl.ds(0, 508)]
        pltpu.make_async_copy(blocks, blocks, ssem.at[n]).wait()
    blocks = s4.at[pl.ds(0, 127)]
    pltpu.make_async_copy(blocks, blocks, ssem.at[3]).wait()


def per_device(
    pair,
    chain_lengths,
    ln_gain,
    ln_bias,
    proj_weight,
    proj_bias,
    out_gain,
    out_bias,
    w_out,
    out_shift,
    w_gate,
    gate_bias,
    cotangent,
):
    def row(v):
        return v.reshape(1, -1)

    vmem = pl.BlockSpec(memory_space=pltpu.VMEM)
    smem = pl.BlockSpec(memory_space=pltpu.SMEM)
    out = jax.ShapeDtypeStruct((4, 128, 128), BF16)
    return pl.pallas_call(
        kernel,
        out_shape=(out, out),
        in_specs=[vmem, smem] + [vmem] * 11,
        out_specs=(vmem, vmem),
        scratch_shapes=[
            pltpu.VMEM((2, 256, 128), BF16),
            pltpu.VMEM((2, 64, 128), BF16),
            pltpu.VMEM((2, 8, 128), F32),
            pltpu.VMEM((8, 128), F32),
            pltpu.VMEM((8, 128, 128), F32),
            pltpu.VMEM((8, 1, 128), F32),
            pltpu.VMEM((8, 128, 128), BF16),
            pltpu.VMEM((1024, 128), F32),
            pltpu.VMEM((64, 16, 128), BF16),
            pltpu.VMEM((64, 16, 128), BF16),
            pltpu.VMEM((1024, 128), F32),
            pltpu.VMEM((256, 256), BF16),
            pltpu.VMEM((256, 256), BF16),
            pltpu.VMEM((512, 128), F32),
            pltpu.VMEM((512, 128), F32),
            pltpu.VMEM((512, 128), F32),
            pltpu.VMEM((512, 128), F32),
            pltpu.VMEM((256, 256), BF16),
            pltpu.VMEM((1024, 128), F32),
            pltpu.VMEM((128, 8, 128), BF16),
            pltpu.VMEM((128, 8, 128), BF16),
            pltpu.VMEM((1024, 128), F32),
            pltpu.VMEM((4, 4, 128, 128), F32),
            pltpu.VMEM((4, 128, 128), F32),
            pltpu.VMEM((4, 128, 128), F32),
            pltpu.VMEM((4, 128, 128), F32),
            pltpu.VMEM((4, 1, 128), F32),
            pltpu.VMEM((4, 128, 128), F32),
            pltpu.VMEM((4, 128, 128), F32),
            pltpu.VMEM((128, 128), BF16),
            pltpu.VMEM((128, 512), BF16),
            pltpu.VMEM((512, 512), BF16),
            pltpu.SemaphoreType.DMA((3,)),
            pltpu.SemaphoreType.DMA((3,)),
            pltpu.SemaphoreType.DMA((4,)),
            pltpu.SemaphoreType.DMA((4,)),
        ],
        compiler_params=pltpu.CompilerParams(
            collective_id=0, has_side_effects=True, vmem_limit_bytes=40 << 20
        ),
    )(
        pair,
        chain_lengths,
        row(ln_gain),
        row(ln_bias),
        proj_weight,
        proj_bias,
        row(out_gain),
        row(out_bias),
        w_out,
        row(out_shift),
        w_gate,
        row(gate_bias),
        cotangent,
    )


def solution(mesh):
    placed = (
        P("dap", None, None),
        P(),
        P(),
        P(),
        P(None, None, "ch"),
        P(None, "ch"),
        P("ch"),
        P("ch"),
        P("ch", None),
        P(),
        P(),
        P(),
        P("dap", "ch", None),
    )
    return jax.shard_map(
        per_device,
        mesh=mesh,
        in_specs=placed,
        out_specs=(P("dap", "ch", None), P("dap", "ch", None)),
        check_vma=False,
    )
```

```python
import jax
import jax.numpy as jnp
from jax import lax
from jax.experimental import pallas as pl
from jax.experimental.pallas import tpu as pltpu
from jax.sharding import PartitionSpec as P

EPS = 1e-05
F32 = jnp.float32
BF16 = jnp.bfloat16
MESH = pl.DeviceIdType.MESH


def sigmoid(x):
    return 0.5 * jnp.tanh(0.5 * x) + 0.5


def mm(a, b):
    return lax.dot_general(a, b, (((1,), (0,)), ((), ())), preferred_element_type=F32)


def mm_nt(a, b):
    return lax.dot_general(a, b, (((1,), (1,)), ((), ())), preferred_element_type=F32)


def mm_tn(a, b):
    return lax.dot_general(a, b, (((0,), (0,)), ((), ())), preferred_element_type=F32)


def column(block, n, rows):
    return jnp.broadcast_to(block[0:rows, n : n + 1], (rows, 128))


def mean0(x):
    return jnp.sum(x, axis=0, keepdims=True) * (1.0 / 128.0)


def hops(n):
    return (0, 1, 2, 1)[n]


STEPS = sorted(
    (
        (dz, dy, dx, dc)
        for dz in range(4)
        for dy in range(4)
        for dx in range(4)
        for dc in range(2)
        if dz + dy + dx + dc
    ),
    key=lambda s: (-hops(s[0]) - hops(s[1]) - hops(s[2]), (s[0] * 5 + s[1] * 3 + s[2]) % 4),
)


def kernel(
    pair_in,
    lens,
    ln_gain_in,
    ln_bias_in,
    pw_in,
    pb_in,
    out_gain_in,
    out_bias_in,
    w_out_in,
    out_shift_in,
    w_gate_in,
    gate_bias_in,
    cot_in,
    update,
    pair_grad,
    pair,
    cot,
    w_gate,
    wt,
    wo,
    hv,
    half,
    vec,
    pnorm,
    pscale,
    normed,
    s1f,
    s1,
    r1,
    r1f,
    lmat,
    rmat,
    s2,
    r2,
    s3f,
    s3,
    r3,
    gmat,
    s4f,
    s4,
    r4,
    r4f,
    factor,
    gate_t,
    cot_t,
    gs_t,
    m1_t,
    tn_t,
    part_t,
    wo_t,
    back_w,
    gp,
    wsem_s,
    wsem_r,
    ssem,
    rsem,
    isem,
):
    p = lax.axis_index("dap")
    g = lax.axis_index("ch")
    me = g * 64 + p

    z, y, x, core = p // 16, p // 4 % 4, p // 2 % 2 * 2 + g, p % 2
    at_z = [(z + n) % 4 * 16 for n in range(4)]
    at_y = [(y + n) % 4 * 4 for n in range(4)]
    at_x = [(x + n) % 4 for n in range(4)]
    at_zy = [[zn + yn for yn in at_y] for zn in at_z]
    at_xc = [[xn // 2 * 2 + c for c in (core, 1 - core)] for xn in at_x]
    at_g = [xn % 2 for xn in at_x]

    def place(step):
        dz, dy, dx, dc = step
        return at_zy[dz][dy] + at_xc[dx][dc], at_g[dx]

    barrier = pltpu.get_barrier_semaphore()
    loads = [
        pltpu.make_async_copy(source, target, isem.at[n])
        for n, (source, target) in enumerate(
            (
                (pair_in, pair),
                (pw_in, wt.at[g]),
                (ln_gain_in, vec.at[0:1]),
                (ln_bias_in, vec.at[1:2]),
                (out_shift_in, vec.at[2:3]),
                (gate_bias_in, vec.at[3:4]),
                (pb_in, half.at[0:4]),
                (out_gain_in, half.at[4:5]),
                (out_bias_in, half.at[5:6]),
                (w_out_in, wo.at[g]),
                (w_gate_in, w_gate),
                (cot_in, cot),
            )
        )
    ]
    for load in loads:
        load.start()
    for step in STEPS:
        pl.semaphore_signal(
            barrier, inc=1, device_id=place(step), device_id_type=MESH
        )
    for load in loads:
        load.wait()

    hv[g] = jnp.zeros((8, 128), F32)
    hv[g, 0:6, 0:64] = half[0:6]
    vcol = vec[...].T
    gain_c = column(vcol, 0, 128)
    bias_c = column(vcol, 1, 128)
    hcol = hv[g].T
    proj_c = [column(hcol, m, 64) for m in range(4)]

    lane = lax.broadcasted_iota(jnp.int32, (1, 128), 1)
    low = lane < 64
    slot = jnp.where(low, lane, lane - 64)

    def present_columns(first_chain):
        limit = jnp.where(low, lens[first_chain], lens[first_chain + 1])
        return jnp.where(slot < limit, 1.0, 0.0)

    row_limit = jnp.full((1, 128), lens[p // 16], jnp.int32)
    row_present = [
        jnp.where(row_limit > lax.rem(p * 4 + i, 64), 1.0, 0.0) for i in range(4)
    ]

    columns = [present_columns(0), present_columns(2)]
    for i in range(4):
        for kh in range(2):
            t = i * 2 + kh
            x = pair[i, kh * 128 : (kh + 1) * 128, :].T.astype(F32)
            mean = mean0(x)
            scale = lax.rsqrt(mean0(x * x) - mean * mean + EPS)
            norm = (x - mean) * scale
            pnorm[t] = norm
            pscale[t] = scale
            nb = (norm * gain_c + bias_c).astype(BF16)
            normed[t] = nb
            mask = row_present[i] * columns[kh]
            pr = mm(wt[g], nb)
            left = sigmoid(pr[0:64] + proj_c[0]) * (pr[64:128] + proj_c[1]) * mask
            right = sigmoid(pr[128:192] + proj_c[2]) * (pr[192:256] + proj_c[3]) * mask
            s1f[pl.ds(i * 4 + kh, 64, stride=16), :] = left
            s1f[pl.ds(i * 4 + 2 + kh, 64, stride=16), :] = right
    s1[...] = s1f[...].reshape(64, 16, 128).astype(BF16)

    gate_w = w_gate[...].T
    gate_c = column(vcol, 3, 128)
    own_columns = present_columns(g * 2)
    for i in range(4):
        gate = sigmoid(mm(gate_w, normed[i * 2 + g]) + gate_c)
        gate_t[i] = gate
        cot_t[i] = cot[i].T.astype(F32)

    pl.semaphore_wait(barrier, 127)

    pltpu.make_async_copy(s1.at[p], r1.at[p], rsem.at[0]).start()
    for step in STEPS:
        if step[2] % 2 == 0:
            t, _ = place(step)
            pltpu.make_async_remote_copy(
                src_ref=s1.at[t],
                dst_ref=r1.at[p],
                send_sem=ssem.at[0],
                recv_sem=rsem.at[0],
                device_id=(t, g),
                device_id_type=MESH,
            ).start()

    swaps = [
        pltpu.make_async_remote_copy(
            src_ref=ref.at[g],
            dst_ref=ref.at[g],
            send_sem=wsem_s.at[n],
            recv_sem=wsem_r.at[n],
            device_id=(p, 1 - g),
            device_id_type=MESH,
        )
        for n, ref in enumerate((wt, wo, hv))
    ]
    for swap in swaps:
        swap.start()

    for swap in swaps:
        swap.wait()
    halves = [hv[0].T, hv[1].T]
    full = [
        jnp.concatenate([column(halves[0], n, 64), column(halves[1], n, 64)], axis=0)
        for n in (4, 5)
    ]
    wo_full = wo[...].reshape(128, 128)
    for i in range(4):
        grad_out = (cot_t[i] * gate_t[i]).astype(BF16)
        gs = mm(wo_full, grad_out) * full[0]
        gs_t[i] = gs
        m1_t[i] = mean0(gs)
    wo_t[...] = wo_full.T
    back_w[...] = wt[...].reshape(512, 128).astype(F32).T.astype(BF16)

    for h in range(2):
        bias = [column(halves[h], m, 64) for m in range(4)]
        rows = slice(h * 64, (h + 1) * 64)
        for i in range(4):
            pr = mm(wt[h], normed[i * 2 + g])
            mask = row_present[i] * own_columns
            for side in range(2):
                n = side * 2
                s = sigmoid(pr[n * 64 : n * 64 + 64] + bias[n])
                sm = s * mask
                value = pr[n * 64 + 64 : n * 64 + 128] + bias[n + 1]
                factor[i, n, rows, :] = value * sm * (1.0 - s)
                factor[i, n + 1, rows, :] = sm

    pltpu.make_async_copy(r1, r1, rsem.at[0]).wait()
    r1f[...] = r1[...].reshape(1024, 128).astype(F32)
    for kh in range(2):
        cols = slice(kh * 128, (kh + 1) * 128)
        lmat[:, cols] = r1f[pl.ds(kh, 256, stride=4), :].astype(BF16)
        rmat[:, cols] = r1f[pl.ds(2 + kh, 256, stride=4), :].astype(BF16)
    for h in range(2):
        s2[h * 256 : (h + 1) * 256, :] = mm_nt(
            lmat[...], rmat[h * 128 : (h + 1) * 128, :]
        )

    def spread(source, target, n, rows):
        def block(ref, t):
            if rows:
                return ref.at[pl.ds(pl.multiple_of(t * rows, rows), rows)]
            return ref.at[t]

        mine = block(target, me)
        pltpu.make_async_copy(block(source, me), mine, rsem.at[n]).start()
        for step in STEPS:
            t, tg = place(step)
            pltpu.make_async_remote_copy(
                src_ref=block(source, tg * 64 + t),
                dst_ref=mine,
                send_sem=ssem.at[n],
                recv_sem=rsem.at[n],
                device_id=(t, tg),
                device_id_type=MESH,
            ).start()

    spread(s2, r2, 1, 4)
    pltpu.make_async_copy(r2, r2, rsem.at[1]).wait()

    for i in range(4):
        tri = r2[pl.ds(i, 128, stride=4), :]
        mean = mean0(tri)
        scale = lax.rsqrt(mean0(tri * tri) - mean * mean + EPS)
        tn = (tri - mean) * scale
        tn_t[i] = tn
        gs = gs_t[i]
        grad = scale * (gs - m1_t[i] - tn * mean0(gs * tn))
        s3f[pl.ds(i, 128, stride=4), :] = grad
    s3[...] = s3f[...].reshape(128, 4, 128).astype(BF16)
    spread(s3, r3, 2, 0)

    shift_c = column(vcol, 2, 128)
    for i in range(4):
        tri_out = (tn_t[i] * full[0] + full[1]).astype(BF16)
        out_sum = mm(wo_t[...], tri_out) + shift_c
        gate = gate_t[i]
        gated = gate * out_sum
        update[i] = gated.T.astype(BF16)
        grad_gate = (cot_t[i] * gated * (1.0 - gate)).astype(BF16)
        part_t[i] = mm(w_gate[...], grad_gate)

    pltpu.make_async_copy(r3, r3, rsem.at[2]).wait()
    for h in range(2):
        part = r3[h * 64 : (h + 1) * 64].astype(F32).reshape(256, 128)
        gmat[:, h * 128 : (h + 1) * 128] = part.astype(BF16)
    grads = (mm(gmat[...], rmat[...]), mm_tn(gmat[...], lmat[...]))
    for side in range(2):
        for h in range(2):
            s4f[pl.ds(h * 512 + side, 256, stride=2), :] = grads[side][
                :, h * 128 : (h + 1) * 128
            ]
    s4[...] = s4f[...].reshape(128, 8, 128).astype(BF16)
    spread(s4, r4, 3, 0)
    pltpu.make_async_copy(r4, r4, rsem.at[3]).wait()

    r4f[...] = r4[...].astype(F32).reshape(1024, 128)
    for i in range(4):
        for side in range(2):
            edge = r4f[pl.ds(i * 2 + side, 128, stride=8), :]
            for n in range(2):
                m = side * 2 + n
                prod = (edge * factor[i, m]).astype(BF16)
                for h in range(2):
                    at = h * 256 + m * 64
                    gp[at : at + 64, i * 128 : (i + 1) * 128] = prod[
                        h * 64 : (h + 1) * 64
                    ]
    for i in range(4):
        grad = mm(back_w[...], gp[:, i * 128 : (i + 1) * 128]) + part_t[i]
        ps = grad * gain_c
        norm = pnorm[i * 2 + g]
        own = pscale[i * 2 + g] * (ps - mean0(ps) - norm * mean0(ps * norm))
        pair_grad[i] = own.T.astype(BF16)

    blocks = s1.at[pl.ds(0, 63)]
    pltpu.make_async_copy(blocks, blocks, ssem.at[0]).wait()
    blocks = s2.at[pl.ds(0, 508)]
    pltpu.make_async_copy(blocks, blocks, ssem.at[1]).wait()
    for n, ref in ((2, s3), (3, s4)):
        blocks = ref.at[pl.ds(0, 127)]
        pltpu.make_async_copy(blocks, blocks, ssem.at[n]).wait()


def per_device(
    pair,
    chain_lengths,
    ln_gain,
    ln_bias,
    proj_weight,
    proj_bias,
    out_gain,
    out_bias,
    w_out,
    out_shift,
    w_gate,
    gate_bias,
    cotangent,
):
    def row(v):
        return v.reshape(1, -1)

    vmem = pl.BlockSpec(memory_space=pltpu.VMEM)
    hbm = pl.BlockSpec(memory_space=pltpu.HBM)
    smem = pl.BlockSpec(memory_space=pltpu.SMEM)
    out = jax.ShapeDtypeStruct((4, 128, 128), BF16)
    return pl.pallas_call(
        kernel,
        out_shape=(out, out),
        in_specs=[hbm, smem] + [hbm] * 11,
        out_specs=(vmem, vmem),
        scratch_shapes=[
            pltpu.VMEM((4, 256, 128), BF16),
            pltpu.VMEM((4, 128, 128), BF16),
            pltpu.VMEM((128, 128), BF16),
            pltpu.VMEM((2, 256, 128), BF16),
            pltpu.VMEM((2, 64, 128), BF16),
            pltpu.VMEM((2, 8, 128), F32),
            pltpu.VMEM((8, 64), F32),
            pltpu.VMEM((8, 128), F32),
            pltpu.VMEM((8, 128, 128), F32),
            pltpu.VMEM((8, 1, 128), F32),
            pltpu.VMEM((8, 128, 128), BF16),
            pltpu.VMEM((1024, 128), F32),
            pltpu.VMEM((64, 16, 128), BF16),
            pltpu.VMEM((64, 16, 128), BF16),
            pltpu.VMEM((1024, 128), F32),
            pltpu.VMEM((256, 256), BF16),
            pltpu.VMEM((256, 256), BF16),
            pltpu.VMEM((512, 128), F32),
            pltpu.VMEM((512, 128), F32),
            pltpu.VMEM((512, 128), F32),
            pltpu.VMEM((128, 4, 128), BF16),
            pltpu.VMEM((128, 4, 128), BF16),
            pltpu.VMEM((256, 256), BF16),
            pltpu.VMEM((1024, 128), F32),
            pltpu.VMEM((128, 8, 128), BF16),
            pltpu.VMEM((128, 8, 128), BF16),
            pltpu.VMEM((1024, 128), F32),
            pltpu.VMEM((4, 4, 128, 128), F32),
            pltpu.VMEM((4, 128, 128), F32),
            pltpu.VMEM((4, 128, 128), F32),
            pltpu.VMEM((4, 128, 128), F32),
            pltpu.VMEM((4, 1, 128), F32),
            pltpu.VMEM((4, 128, 128), F32),
            pltpu.VMEM((4, 128, 128), F32),
            pltpu.VMEM((128, 128), BF16),
            pltpu.VMEM((128, 512), BF16),
            pltpu.VMEM((512, 512), BF16),
            pltpu.SemaphoreType.DMA((3,)),
            pltpu.SemaphoreType.DMA((3,)),
            pltpu.SemaphoreType.DMA((4,)),
            pltpu.SemaphoreType.DMA((4,)),
            pltpu.SemaphoreType.DMA((12,)),
        ],
        compiler_params=pltpu.CompilerParams(
            collective_id=0, has_side_effects=True, vmem_limit_bytes=63 << 20
        ),
    )(
        pair,
        chain_lengths,
        row(ln_gain),
        row(ln_bias),
        jnp.swapaxes(proj_weight, 1, 2).reshape(256, 128),
        proj_bias,
        row(out_gain),
        row(out_bias),
        w_out,
        row(out_shift),
        w_gate,
        row(gate_bias),
        cotangent,
    )


def solution(mesh):
    placed = (
        P("dap", None, None),
        P(),
        P(),
        P(),
        P(None, None, "ch"),
        P(None, "ch"),
        P("ch"),
        P("ch"),
        P("ch", None),
        P(),
        P(),
        P(),
        P("dap", "ch", None),
    )
    return jax.shard_map(
        per_device,
        mesh=mesh,
        in_specs=placed,
        out_specs=(P("dap", "ch", None), P("dap", "ch", None)),
        check_vma=False,
    )
```

```python
import jax
import jax.numpy as jnp
from jax import lax
from jax.experimental import pallas as pl
from jax.experimental.pallas import tpu as pltpu
from jax.sharding import PartitionSpec as P

EPS = 1e-05
F32 = jnp.float32
BF16 = jnp.bfloat16
MESH = pl.DeviceIdType.MESH


def sigmoid(x):
    return 0.5 * jnp.tanh(0.5 * x) + 0.5


def mm(a, b):
    return lax.dot_general(a, b, (((1,), (0,)), ((), ())), preferred_element_type=F32)


def mm_nt(a, b):
    return lax.dot_general(a, b, (((1,), (1,)), ((), ())), preferred_element_type=F32)


def mm_tn(a, b):
    return lax.dot_general(a, b, (((0,), (0,)), ((), ())), preferred_element_type=F32)


def column(block, n, rows):
    return jnp.broadcast_to(block[0:rows, n : n + 1], (rows, 128))


def mean0(x):
    return jnp.sum(x, axis=0, keepdims=True) * (1.0 / 128.0)


def hops(n):
    return (0, 1, 2, 1)[n]


STEPS = sorted(
    (
        (dz, dy, dx, dc)
        for dz in range(4)
        for dy in range(4)
        for dx in range(4)
        for dc in range(2)
        if dz + dy + dx + dc
    ),
    key=lambda s: (-hops(s[0]) - hops(s[1]) - hops(s[2]), (s[0] * 5 + s[1] * 3 + s[2]) % 4),
)


def kernel(
    pair_in,
    lens,
    ln_gain_in,
    ln_bias_in,
    pw_in,
    pb_in,
    out_gain_in,
    out_bias_in,
    w_out_in,
    out_shift_in,
    w_gate_in,
    gate_bias_in,
    cot_in,
    outs,
    pair,
    cot,
    w_gate,
    wt,
    wo,
    hv,
    half,
    vec,
    pnorm,
    pscale,
    normed,
    s1f,
    s1,
    r1,
    r1f,
    lmat,
    rmat,
    s2,
    r2,
    s3f,
    s3,
    r3,
    gmat,
    s4f,
    s4,
    r4,
    r4f,
    factor,
    gate_t,
    cot_t,
    gs_t,
    m1_t,
    tn_t,
    part_t,
    wo_t,
    back_w,
    gp,
    wsem_s,
    wsem_r,
    ssem,
    rsem,
    isem,
):
    p = lax.axis_index("dap")
    g = lax.axis_index("ch")
    me = g * 64 + p

    z, y, x, core = p // 16, p // 4 % 4, p // 2 % 2 * 2 + g, p % 2
    at_z = [(z + n) % 4 * 16 for n in range(4)]
    at_y = [(y + n) % 4 * 4 for n in range(4)]
    at_x = [(x + n) % 4 for n in range(4)]
    at_zy = [[zn + yn for yn in at_y] for zn in at_z]
    at_xc = [[xn // 2 * 2 + c for c in (core, 1 - core)] for xn in at_x]
    at_g = [xn % 2 for xn in at_x]

    def place(step):
        dz, dy, dx, dc = step
        return at_zy[dz][dy] + at_xc[dx][dc], at_g[dx]

    barrier = pltpu.get_barrier_semaphore()
    for step in STEPS:
        pl.semaphore_signal(
            barrier, inc=1, device_id=place(step), device_id_type=MESH
        )
    loads = [
        pltpu.make_async_copy(source, target, isem.at[n])
        for n, (source, target) in enumerate(
            (
                (pair_in, pair),
                (pw_in, wt.at[g]),
                (ln_gain_in, vec.at[0:1]),
                (ln_bias_in, vec.at[1:2]),
                (out_shift_in, vec.at[2:3]),
                (gate_bias_in, vec.at[3:4]),
                (pb_in, half.at[0:4]),
                (out_gain_in, half.at[4:5]),
                (out_bias_in, half.at[5:6]),
                (w_out_in, wo.at[g]),
                (w_gate_in, w_gate),
                (cot_in, cot),
            )
        )
    ]
    for load in loads:
        load.start()
    for load in loads:
        load.wait()

    hv[g] = jnp.zeros((8, 128), F32)
    hv[g, 0:6, 0:64] = half[0:6]
    vcol = vec[...].T
    gain_c = column(vcol, 0, 128)
    bias_c = column(vcol, 1, 128)
    hcol = hv[g].T
    proj_c = [column(hcol, m, 64) for m in range(4)]

    lane = lax.broadcasted_iota(jnp.int32, (1, 128), 1)
    low = lane < 64
    slot = jnp.where(low, lane, lane - 64)

    def present_columns(first_chain):
        limit = jnp.where(low, lens[first_chain], lens[first_chain + 1])
        return jnp.where(slot < limit, 1.0, 0.0)

    row_limit = jnp.full((1, 128), lens[p // 16], jnp.int32)
    row_present = [
        jnp.where(row_limit > lax.rem(p * 4 + i, 64), 1.0, 0.0) for i in range(4)
    ]

    columns = [present_columns(0), present_columns(2)]
    for i in range(4):
        for kh in range(2):
            t = i * 2 + kh
            x = pair[i, kh * 128 : (kh + 1) * 128, :].T.astype(F32)
            mean = mean0(x)
            scale = lax.rsqrt(mean0(x * x) - mean * mean + EPS)
            norm = (x - mean) * scale
            pnorm[t] = norm
            pscale[t] = scale
            nb = (norm * gain_c + bias_c).astype(BF16)
            normed[t] = nb
            mask = row_present[i] * columns[kh]
            pr = mm(wt[g], nb)
            left = sigmoid(pr[0:64] + proj_c[0]) * (pr[64:128] + proj_c[1]) * mask
            right = sigmoid(pr[128:192] + proj_c[2]) * (pr[192:256] + proj_c[3]) * mask
            s1f[pl.ds(i * 4 + kh, 64, stride=16), :] = left
            s1f[pl.ds(i * 4 + 2 + kh, 64, stride=16), :] = right
    s1[...] = s1f[...].reshape(64, 16, 128).astype(BF16)

    gate_w = w_gate[...].T
    gate_c = column(vcol, 3, 128)
    own_columns = present_columns(g * 2)
    for i in range(4):
        gate = sigmoid(mm(gate_w, normed[i * 2 + g]) + gate_c)
        gate_t[i] = gate
        cot_t[i] = cot[i].T.astype(F32)

    pl.semaphore_wait(barrier, 127)

    pltpu.make_async_copy(s1.at[p], r1.at[p], rsem.at[0]).start()
    for step in STEPS:
        if step[2] % 2 == 0:
            t, _ = place(step)
            pltpu.make_async_remote_copy(
                src_ref=s1.at[t],
                dst_ref=r1.at[p],
                send_sem=ssem.at[0],
                recv_sem=rsem.at[0],
                device_id=(t, g),
                device_id_type=MESH,
            ).start()

    swaps = [
        pltpu.make_async_remote_copy(
            src_ref=ref.at[g],
            dst_ref=ref.at[g],
            send_sem=wsem_s.at[n],
            recv_sem=wsem_r.at[n],
            device_id=(p, 1 - g),
            device_id_type=MESH,
        )
        for n, ref in enumerate((wt, wo, hv))
    ]
    for swap in swaps:
        swap.start()

    for swap in swaps:
        swap.wait()
    halves = [hv[0].T, hv[1].T]
    full = [
        jnp.concatenate([column(halves[0], n, 64), column(halves[1], n, 64)], axis=0)
        for n in (4, 5)
    ]
    wo_full = wo[...].reshape(128, 128)
    for i in range(4):
        grad_out = (cot_t[i] * gate_t[i]).astype(BF16)
        gs = mm(wo_full, grad_out) * full[0]
        gs_t[i] = gs
        m1_t[i] = mean0(gs)
    wo_t[...] = wo_full.T
    back_w[...] = wt[...].reshape(512, 128).astype(F32).T.astype(BF16)

    for h in range(2):
        bias = [column(halves[h], m, 64) for m in range(4)]
        rows = slice(h * 64, (h + 1) * 64)
        for i in range(4):
            pr = mm(wt[h], normed[i * 2 + g])
            mask = row_present[i] * own_columns
            for side in range(2):
                n = side * 2
                s = sigmoid(pr[n * 64 : n * 64 + 64] + bias[n])
                sm = s * mask
                value = pr[n * 64 + 64 : n * 64 + 128] + bias[n + 1]
                factor[i, n, rows, :] = value * sm * (1.0 - s)
                factor[i, n + 1, rows, :] = sm

    pltpu.make_async_copy(r1, r1, rsem.at[0]).wait()
    r1f[...] = r1[...].reshape(1024, 128).astype(F32)
    for kh in range(2):
        cols = slice(kh * 128, (kh + 1) * 128)
        lmat[:, cols] = r1f[pl.ds(kh, 256, stride=4), :].astype(BF16)
        rmat[:, cols] = r1f[pl.ds(2 + kh, 256, stride=4), :].astype(BF16)
    for h in range(2):
        s2[h * 256 : (h + 1) * 256, :] = mm_nt(
            lmat[...], rmat[h * 128 : (h + 1) * 128, :]
        )

    def spread(source, target, n, rows):
        def block(ref, t):
            if rows:
                return ref.at[pl.ds(pl.multiple_of(t * rows, rows), rows)]
            return ref.at[t]

        mine = block(target, me)
        pltpu.make_async_copy(block(source, me), mine, rsem.at[n]).start()
        for step in STEPS:
            t, tg = place(step)
            pltpu.make_async_remote_copy(
                src_ref=block(source, tg * 64 + t),
                dst_ref=mine,
                send_sem=ssem.at[n],
                recv_sem=rsem.at[n],
                device_id=(t, tg),
                device_id_type=MESH,
            ).start()

    spread(s2, r2, 1, 4)
    pltpu.make_async_copy(r2, r2, rsem.at[1]).wait()

    for i in range(4):
        tri = r2[pl.ds(i, 128, stride=4), :]
        mean = mean0(tri)
        scale = lax.rsqrt(mean0(tri * tri) - mean * mean + EPS)
        tn = (tri - mean) * scale
        tn_t[i] = tn
        gs = gs_t[i]
        grad = scale * (gs - m1_t[i] - tn * mean0(gs * tn))
        s3f[pl.ds(i, 128, stride=4), :] = grad
    s3[...] = s3f[...].reshape(128, 4, 128).astype(BF16)
    spread(s3, r3, 2, 0)

    shift_c = column(vcol, 2, 128)
    for i in range(4):
        tri_out = (tn_t[i] * full[0] + full[1]).astype(BF16)
        out_sum = mm(wo_t[...], tri_out) + shift_c
        gate = gate_t[i]
        gated = gate * out_sum
        outs[0, i] = gated.T.astype(BF16)
        grad_gate = (cot_t[i] * gated * (1.0 - gate)).astype(BF16)
        part_t[i] = mm(w_gate[...], grad_gate)

    pltpu.make_async_copy(r3, r3, rsem.at[2]).wait()
    for h in range(2):
        part = r3[h * 64 : (h + 1) * 64].astype(F32).reshape(256, 128)
        gmat[:, h * 128 : (h + 1) * 128] = part.astype(BF16)
    grads = (mm(gmat[...], rmat[...]), mm_tn(gmat[...], lmat[...]))
    for side in range(2):
        for h in range(2):
            s4f[pl.ds(h * 512 + side, 256, stride=2), :] = grads[side][
                :, h * 128 : (h + 1) * 128
            ]
    s4[...] = s4f[...].reshape(128, 8, 128).astype(BF16)
    spread(s4, r4, 3, 0)
    pltpu.make_async_copy(r4, r4, rsem.at[3]).wait()

    r4f[...] = r4[...].astype(F32).reshape(1024, 128)
    for i in range(4):
        for side in range(2):
            edge = r4f[pl.ds(i * 2 + side, 128, stride=8), :]
            for n in range(2):
                m = side * 2 + n
                prod = (edge * factor[i, m]).astype(BF16)
                for h in range(2):
                    at = h * 256 + m * 64
                    gp[at : at + 64, i * 128 : (i + 1) * 128] = prod[
                        h * 64 : (h + 1) * 64
                    ]
    for i in range(4):
        grad = mm(back_w[...], gp[:, i * 128 : (i + 1) * 128]) + part_t[i]
        ps = grad * gain_c
        norm = pnorm[i * 2 + g]
        own = pscale[i * 2 + g] * (ps - mean0(ps) - norm * mean0(ps * norm))
        outs[1, i] = own.T.astype(BF16)

    blocks = s1.at[pl.ds(0, 63)]
    pltpu.make_async_copy(blocks, blocks, ssem.at[0]).wait()
    blocks = s2.at[pl.ds(0, 508)]
    pltpu.make_async_copy(blocks, blocks, ssem.at[1]).wait()
    for n, ref in ((2, s3), (3, s4)):
        blocks = ref.at[pl.ds(0, 127)]
        pltpu.make_async_copy(blocks, blocks, ssem.at[n]).wait()


def publish(outs, update, pair_grad, sem):
    copies = [
        pltpu.make_async_copy(outs.at[n], target, sem.at[n])
        for n, target in enumerate((update, pair_grad))
    ]
    for copy in copies:
        copy.start()
    for copy in copies:
        copy.wait()


def per_device(
    pair,
    chain_lengths,
    ln_gain,
    ln_bias,
    proj_weight,
    proj_bias,
    out_gain,
    out_bias,
    w_out,
    out_shift,
    w_gate,
    gate_bias,
    cotangent,
):
    def row(v):
        return v.reshape(1, -1)

    vmem = pl.BlockSpec(memory_space=pltpu.VMEM)
    hbm = pl.BlockSpec(memory_space=pltpu.HBM)
    smem = pl.BlockSpec(memory_space=pltpu.SMEM)
    out = jax.ShapeDtypeStruct((4, 128, 128), BF16)
    outs = pl.pallas_call(
        kernel,
        out_shape=jax.ShapeDtypeStruct((2, 4, 128, 128), BF16),
        in_specs=[hbm, smem] + [hbm] * 11,
        out_specs=vmem,
        scratch_shapes=[
            pltpu.VMEM((4, 256, 128), BF16),
            pltpu.VMEM((4, 128, 128), BF16),
            pltpu.VMEM((128, 128), BF16),
            pltpu.VMEM((2, 256, 128), BF16),
            pltpu.VMEM((2, 64, 128), BF16),
            pltpu.VMEM((2, 8, 128), F32),
            pltpu.VMEM((8, 64), F32),
            pltpu.VMEM((8, 128), F32),
            pltpu.VMEM((8, 128, 128), F32),
            pltpu.VMEM((8, 1, 128), F32),
            pltpu.VMEM((8, 128, 128), BF16),
            pltpu.VMEM((1024, 128), F32),
            pltpu.VMEM((64, 16, 128), BF16),
            pltpu.VMEM((64, 16, 128), BF16),
            pltpu.VMEM((1024, 128), F32),
            pltpu.VMEM((256, 256), BF16),
            pltpu.VMEM((256, 256), BF16),
            pltpu.VMEM((512, 128), F32),
            pltpu.VMEM((512, 128), F32),
            pltpu.VMEM((512, 128), F32),
            pltpu.VMEM((128, 4, 128), BF16),
            pltpu.VMEM((128, 4, 128), BF16),
            pltpu.VMEM((256, 256), BF16),
            pltpu.VMEM((1024, 128), F32),
            pltpu.VMEM((128, 8, 128), BF16),
            pltpu.VMEM((128, 8, 128), BF16),
            pltpu.VMEM((1024, 128), F32),
            pltpu.VMEM((4, 4, 128, 128), F32),
            pltpu.VMEM((4, 128, 128), F32),
            pltpu.VMEM((4, 128, 128), F32),
            pltpu.VMEM((4, 128, 128), F32),
            pltpu.VMEM((4, 1, 128), F32),
            pltpu.VMEM((4, 128, 128), F32),
            pltpu.VMEM((4, 128, 128), F32),
            pltpu.VMEM((128, 128), BF16),
            pltpu.VMEM((128, 512), BF16),
            pltpu.VMEM((512, 512), BF16),
            pltpu.SemaphoreType.DMA((3,)),
            pltpu.SemaphoreType.DMA((3,)),
            pltpu.SemaphoreType.DMA((4,)),
            pltpu.SemaphoreType.DMA((4,)),
            pltpu.SemaphoreType.DMA((12,)),
        ],
        compiler_params=pltpu.CompilerParams(
            collective_id=0, has_side_effects=True, vmem_limit_bytes=63 << 20
        ),
    )(
        pair,
        chain_lengths,
        row(ln_gain),
        row(ln_bias),
        jnp.swapaxes(proj_weight, 1, 2).reshape(256, 128),
        proj_bias,
        row(out_gain),
        row(out_bias),
        w_out,
        row(out_shift),
        w_gate,
        row(gate_bias),
        cotangent,
    )
    return pl.pallas_call(
        publish,
        out_shape=(out, out),
        in_specs=[vmem],
        out_specs=(hbm, hbm),
        scratch_shapes=[pltpu.SemaphoreType.DMA((2,))],
    )(outs)


def solution(mesh):
    placed = (
        P("dap", None, None),
        P(),
        P(),
        P(),
        P(None, None, "ch"),
        P(None, "ch"),
        P("ch"),
        P("ch"),
        P("ch", None),
        P(),
        P(),
        P(),
        P("dap", "ch", None),
    )
    return jax.shard_map(
        per_device,
        mesh=mesh,
        in_specs=placed,
        out_specs=(P("dap", "ch", None), P("dap", "ch", None)),
        check_vma=False,
    )
```

```python
import random

import jax
import jax.numpy as jnp
from jax import lax
from jax.experimental import pallas as pl
from jax.experimental.pallas import tpu as pltpu
from jax.sharding import PartitionSpec as P

EPS = 1e-05
F32 = jnp.float32
BF16 = jnp.bfloat16
MESH = pl.DeviceIdType.MESH


def sigmoid(x):
    return 0.5 * jnp.tanh(0.5 * x) + 0.5


def mm(a, b):
    return lax.dot_general(a, b, (((1,), (0,)), ((), ())), preferred_element_type=F32)


def mm_nt(a, b):
    return lax.dot_general(a, b, (((1,), (1,)), ((), ())), preferred_element_type=F32)


def mm_tn(a, b):
    return lax.dot_general(a, b, (((0,), (0,)), ((), ())), preferred_element_type=F32)


def column(block, n, rows):
    return jnp.broadcast_to(block[0:rows, n : n + 1], (rows, 128))


def mean0(x):
    return jnp.sum(x, axis=0, keepdims=True) * (1.0 / 128.0)


def hops(n):
    return (0, 1, 2, 1)[n]


STEPS = [
    (dz, dy, dx, dc)
    for dz in range(4)
    for dy in range(4)
    for dx in range(4)
    for dc in range(2)
    if dz + dy + dx + dc
]
random.Random(1).shuffle(STEPS)
STEPS.sort(key=lambda s: -hops(s[0]) - hops(s[1]) - hops(s[2]))


def kernel(
    pair_in,
    lens,
    ln_gain_in,
    ln_bias_in,
    pw_in,
    pb_in,
    out_gain_in,
    out_bias_in,
    w_out_in,
    out_shift_in,
    w_gate_in,
    gate_bias_in,
    cot_in,
    outs,
    pair,
    cot,
    w_gate,
    wt,
    wo,
    hv,
    half,
    vec,
    pnorm,
    pscale,
    normed,
    s1f,
    s1,
    r1,
    r1f,
    lmat,
    rmat,
    s2,
    r2,
    s3f,
    s3,
    r3,
    gmat,
    s4f,
    s4,
    r4,
    r4f,
    factor,
    gate_t,
    cot_t,
    gs_t,
    m1_t,
    tn_t,
    part_t,
    wo_t,
    back_w,
    gp,
    wsem_s,
    wsem_r,
    ssem,
    rsem,
    isem,
):
    p = lax.axis_index("dap")
    g = lax.axis_index("ch")
    me = g * 64 + p

    z, y, x, core = p // 16, p // 4 % 4, p // 2 % 2 * 2 + g, p % 2
    at_z = [(z + n) % 4 * 16 for n in range(4)]
    at_y = [(y + n) % 4 * 4 for n in range(4)]
    at_x = [(x + n) % 4 for n in range(4)]
    at_zy = [[zn + yn for yn in at_y] for zn in at_z]
    at_xc = [[xn // 2 * 2 + c for c in (core, 1 - core)] for xn in at_x]
    at_g = [xn % 2 for xn in at_x]

    def place(step):
        dz, dy, dx, dc = step
        return at_zy[dz][dy] + at_xc[dx][dc], at_g[dx]

    barrier = pltpu.get_barrier_semaphore()
    for step in STEPS:
        pl.semaphore_signal(
            barrier, inc=1, device_id=place(step), device_id_type=MESH
        )
    loads = [
        pltpu.make_async_copy(source, target, isem.at[n])
        for n, (source, target) in enumerate(
            (
                (pair_in, pair),
                (pw_in, wt.at[g]),
                (ln_gain_in, vec.at[0:1]),
                (ln_bias_in, vec.at[1:2]),
                (out_shift_in, vec.at[2:3]),
                (gate_bias_in, vec.at[3:4]),
                (pb_in, half.at[0:4]),
                (out_gain_in, half.at[4:5]),
                (out_bias_in, half.at[5:6]),
                (w_out_in, wo.at[g]),
                (w_gate_in, w_gate),
                (cot_in, cot),
            )
        )
    ]
    for load in loads:
        load.start()
    for load in loads:
        load.wait()

    hv[g] = jnp.zeros((8, 128), F32)
    hv[g, 0:6, 0:64] = half[0:6]
    vcol = vec[...].T
    gain_c = column(vcol, 0, 128)
    bias_c = column(vcol, 1, 128)
    hcol = hv[g].T
    proj_c = [column(hcol, m, 64) for m in range(4)]

    lane = lax.broadcasted_iota(jnp.int32, (1, 128), 1)
    low = lane < 64
    slot = jnp.where(low, lane, lane - 64)

    def present_columns(first_chain):
        limit = jnp.where(low, lens[first_chain], lens[first_chain + 1])
        return jnp.where(slot < limit, 1.0, 0.0)

    row_limit = jnp.full((1, 128), lens[p // 16], jnp.int32)
    row_present = [
        jnp.where(row_limit > lax.rem(p * 4 + i, 64), 1.0, 0.0) for i in range(4)
    ]

    columns = [present_columns(0), present_columns(2)]
    for i in range(4):
        for kh in range(2):
            t = i * 2 + kh
            x = pair[i, kh * 128 : (kh + 1) * 128, :].T.astype(F32)
            mean = mean0(x)
            scale = lax.rsqrt(mean0(x * x) - mean * mean + EPS)
            norm = (x - mean) * scale
            pnorm[t] = norm
            pscale[t] = scale
            nb = (norm * gain_c + bias_c).astype(BF16)
            normed[t] = nb
            mask = row_present[i] * columns[kh]
            pr = mm(wt[g], nb)
            left = sigmoid(pr[0:64] + proj_c[0]) * (pr[64:128] + proj_c[1]) * mask
            right = sigmoid(pr[128:192] + proj_c[2]) * (pr[192:256] + proj_c[3]) * mask
            s1f[pl.ds(i * 4 + kh, 64, stride=16), :] = left
            s1f[pl.ds(i * 4 + 2 + kh, 64, stride=16), :] = right
    s1[...] = s1f[...].reshape(64, 16, 128).astype(BF16)

    gate_w = w_gate[...].T
    gate_c = column(vcol, 3, 128)
    own_columns = present_columns(g * 2)
    for i in range(4):
        gate = sigmoid(mm(gate_w, normed[i * 2 + g]) + gate_c)
        gate_t[i] = gate
        cot_t[i] = cot[i].T.astype(F32)

    pl.semaphore_wait(barrier, 127)

    pltpu.make_async_copy(s1.at[p], r1.at[p], rsem.at[0]).start()
    for step in STEPS:
        if step[2] % 2 == 0:
            t, _ = place(step)
            pltpu.make_async_remote_copy(
                src_ref=s1.at[t],
                dst_ref=r1.at[p],
                send_sem=ssem.at[0],
                recv_sem=rsem.at[0],
                device_id=(t, g),
                device_id_type=MESH,
            ).start()

    swaps = [
        pltpu.make_async_remote_copy(
            src_ref=ref.at[g],
            dst_ref=ref.at[g],
            send_sem=wsem_s.at[n],
            recv_sem=wsem_r.at[n],
            device_id=(p, 1 - g),
            device_id_type=MESH,
        )
        for n, ref in enumerate((wt, wo, hv))
    ]
    for swap in swaps:
        swap.start()

    for swap in swaps:
        swap.wait()
    halves = [hv[0].T, hv[1].T]
    full = [
        jnp.concatenate([column(halves[0], n, 64), column(halves[1], n, 64)], axis=0)
        for n in (4, 5)
    ]
    wo_full = wo[...].reshape(128, 128)
    for i in range(4):
        grad_out = (cot_t[i] * gate_t[i]).astype(BF16)
        gs = mm(wo_full, grad_out) * full[0]
        gs_t[i] = gs
        m1_t[i] = mean0(gs)
    wo_t[...] = wo_full.T
    back_w[...] = wt[...].reshape(512, 128).astype(F32).T.astype(BF16)

    for h in range(2):
        bias = [column(halves[h], m, 64) for m in range(4)]
        rows = slice(h * 64, (h + 1) * 64)
        for i in range(4):
            pr = mm(wt[h], normed[i * 2 + g])
            mask = row_present[i] * own_columns
            for side in range(2):
                n = side * 2
                s = sigmoid(pr[n * 64 : n * 64 + 64] + bias[n])
                sm = s * mask
                value = pr[n * 64 + 64 : n * 64 + 128] + bias[n + 1]
                factor[i, n, rows, :] = value * sm * (1.0 - s)
                factor[i, n + 1, rows, :] = sm

    pltpu.make_async_copy(r1, r1, rsem.at[0]).wait()
    r1f[...] = r1[...].reshape(1024, 128).astype(F32)
    for kh in range(2):
        cols = slice(kh * 128, (kh + 1) * 128)
        lmat[:, cols] = r1f[pl.ds(kh, 256, stride=4), :].astype(BF16)
        rmat[:, cols] = r1f[pl.ds(2 + kh, 256, stride=4), :].astype(BF16)
    for h in range(2):
        s2[h * 256 : (h + 1) * 256, :] = mm_nt(
            lmat[...], rmat[h * 128 : (h + 1) * 128, :]
        )

    def spread(source, target, n, rows):
        def block(ref, t):
            if rows:
                return ref.at[pl.ds(pl.multiple_of(t * rows, rows), rows)]
            return ref.at[t]

        mine = block(target, me)
        pltpu.make_async_copy(block(source, me), mine, rsem.at[n]).start()
        for step in STEPS:
            t, tg = place(step)
            pltpu.make_async_remote_copy(
                src_ref=block(source, tg * 64 + t),
                dst_ref=mine,
                send_sem=ssem.at[n],
                recv_sem=rsem.at[n],
                device_id=(t, tg),
                device_id_type=MESH,
            ).start()

    spread(s2, r2, 1, 4)
    pltpu.make_async_copy(r2, r2, rsem.at[1]).wait()

    for i in range(4):
        tri = r2[pl.ds(i, 128, stride=4), :]
        mean = mean0(tri)
        scale = lax.rsqrt(mean0(tri * tri) - mean * mean + EPS)
        tn = (tri - mean) * scale
        tn_t[i] = tn
        gs = gs_t[i]
        grad = scale * (gs - m1_t[i] - tn * mean0(gs * tn))
        s3f[pl.ds(i, 128, stride=4), :] = grad
    s3[...] = s3f[...].reshape(128, 4, 128).astype(BF16)
    spread(s3, r3, 2, 0)

    shift_c = column(vcol, 2, 128)
    for i in range(4):
        tri_out = (tn_t[i] * full[0] + full[1]).astype(BF16)
        out_sum = mm(wo_t[...], tri_out) + shift_c
        gate = gate_t[i]
        gated = gate * out_sum
        outs[0, i] = gated.T.astype(BF16)
        grad_gate = (cot_t[i] * gated * (1.0 - gate)).astype(BF16)
        part_t[i] = mm(w_gate[...], grad_gate)

    pltpu.make_async_copy(r3, r3, rsem.at[2]).wait()
    for h in range(2):
        part = r3[h * 64 : (h + 1) * 64].astype(F32).reshape(256, 128)
        gmat[:, h * 128 : (h + 1) * 128] = part.astype(BF16)
    grads = (mm(gmat[...], rmat[...]), mm_tn(gmat[...], lmat[...]))
    for side in range(2):
        for h in range(2):
            s4f[pl.ds(h * 512 + side, 256, stride=2), :] = grads[side][
                :, h * 128 : (h + 1) * 128
            ]
    s4[...] = s4f[...].reshape(128, 8, 128).astype(BF16)
    spread(s4, r4, 3, 0)
    pltpu.make_async_copy(r4, r4, rsem.at[3]).wait()

    r4f[...] = r4[...].astype(F32).reshape(1024, 128)
    for i in range(4):
        for side in range(2):
            edge = r4f[pl.ds(i * 2 + side, 128, stride=8), :]
            for n in range(2):
                m = side * 2 + n
                prod = (edge * factor[i, m]).astype(BF16)
                for h in range(2):
                    at = h * 256 + m * 64
                    gp[at : at + 64, i * 128 : (i + 1) * 128] = prod[
                        h * 64 : (h + 1) * 64
                    ]
    for i in range(4):
        grad = mm(back_w[...], gp[:, i * 128 : (i + 1) * 128]) + part_t[i]
        ps = grad * gain_c
        norm = pnorm[i * 2 + g]
        own = pscale[i * 2 + g] * (ps - mean0(ps) - norm * mean0(ps * norm))
        outs[1, i] = own.T.astype(BF16)

    blocks = s1.at[pl.ds(0, 63)]
    pltpu.make_async_copy(blocks, blocks, ssem.at[0]).wait()
    blocks = s2.at[pl.ds(0, 508)]
    pltpu.make_async_copy(blocks, blocks, ssem.at[1]).wait()
    for n, ref in ((2, s3), (3, s4)):
        blocks = ref.at[pl.ds(0, 127)]
        pltpu.make_async_copy(blocks, blocks, ssem.at[n]).wait()


def publish(outs, update, pair_grad, sem):
    copies = [
        pltpu.make_async_copy(outs.at[n], target, sem.at[n])
        for n, target in enumerate((update, pair_grad))
    ]
    for copy in copies:
        copy.start()
    for copy in copies:
        copy.wait()


def per_device(
    pair,
    chain_lengths,
    ln_gain,
    ln_bias,
    proj_weight,
    proj_bias,
    out_gain,
    out_bias,
    w_out,
    out_shift,
    w_gate,
    gate_bias,
    cotangent,
):
    def row(v):
        return v.reshape(1, -1)

    vmem = pl.BlockSpec(memory_space=pltpu.VMEM)
    hbm = pl.BlockSpec(memory_space=pltpu.HBM)
    smem = pl.BlockSpec(memory_space=pltpu.SMEM)
    out = jax.ShapeDtypeStruct((4, 128, 128), BF16)
    outs = pl.pallas_call(
        kernel,
        out_shape=jax.ShapeDtypeStruct((2, 4, 128, 128), BF16),
        in_specs=[hbm, smem] + [hbm] * 11,
        out_specs=vmem,
        scratch_shapes=[
            pltpu.VMEM((4, 256, 128), BF16),
            pltpu.VMEM((4, 128, 128), BF16),
            pltpu.VMEM((128, 128), BF16),
            pltpu.VMEM((2, 256, 128), BF16),
            pltpu.VMEM((2, 64, 128), BF16),
            pltpu.VMEM((2, 8, 128), F32),
            pltpu.VMEM((8, 64), F32),
            pltpu.VMEM((8, 128), F32),
            pltpu.VMEM((8, 128, 128), F32),
            pltpu.VMEM((8, 1, 128), F32),
            pltpu.VMEM((8, 128, 128), BF16),
            pltpu.VMEM((1024, 128), F32),
            pltpu.VMEM((64, 16, 128), BF16),
            pltpu.VMEM((64, 16, 128), BF16),
            pltpu.VMEM((1024, 128), F32),
            pltpu.VMEM((256, 256), BF16),
            pltpu.VMEM((256, 256), BF16),
            pltpu.VMEM((512, 128), F32),
            pltpu.VMEM((512, 128), F32),
            pltpu.VMEM((512, 128), F32),
            pltpu.VMEM((128, 4, 128), BF16),
            pltpu.VMEM((128, 4, 128), BF16),
            pltpu.VMEM((256, 256), BF16),
            pltpu.VMEM((1024, 128), F32),
            pltpu.VMEM((128, 8, 128), BF16),
            pltpu.VMEM((128, 8, 128), BF16),
            pltpu.VMEM((1024, 128), F32),
            pltpu.VMEM((4, 4, 128, 128), F32),
            pltpu.VMEM((4, 128, 128), F32),
            pltpu.VMEM((4, 128, 128), F32),
            pltpu.VMEM((4, 128, 128), F32),
            pltpu.VMEM((4, 1, 128), F32),
            pltpu.VMEM((4, 128, 128), F32),
            pltpu.VMEM((4, 128, 128), F32),
            pltpu.VMEM((128, 128), BF16),
            pltpu.VMEM((128, 512), BF16),
            pltpu.VMEM((512, 512), BF16),
            pltpu.SemaphoreType.DMA((3,)),
            pltpu.SemaphoreType.DMA((3,)),
            pltpu.SemaphoreType.DMA((4,)),
            pltpu.SemaphoreType.DMA((4,)),
            pltpu.SemaphoreType.DMA((12,)),
        ],
        compiler_params=pltpu.CompilerParams(
            collective_id=0, has_side_effects=True, vmem_limit_bytes=63 << 20
        ),
    )(
        pair,
        chain_lengths,
        row(ln_gain),
        row(ln_bias),
        jnp.swapaxes(proj_weight, 1, 2).reshape(256, 128),
        proj_bias,
        row(out_gain),
        row(out_bias),
        w_out,
        row(out_shift),
        w_gate,
        row(gate_bias),
        cotangent,
    )
    return pl.pallas_call(
        publish,
        out_shape=(out, out),
        in_specs=[vmem],
        out_specs=(hbm, hbm),
        scratch_shapes=[pltpu.SemaphoreType.DMA((2,))],
    )(outs)


def solution(mesh):
    placed = (
        P("dap", None, None),
        P(),
        P(),
        P(),
        P(None, None, "ch"),
        P(None, "ch"),
        P("ch"),
        P("ch"),
        P("ch", None),
        P(),
        P(),
        P(),
        P("dap", "ch", None),
    )
    return jax.shard_map(
        per_device,
        mesh=mesh,
        in_specs=placed,
        out_specs=(P("dap", "ch", None), P("dap", "ch", None)),
        check_vma=False,
    )
```

```python
import random

import jax
import jax.numpy as jnp
from jax import lax
from jax.experimental import pallas as pl
from jax.experimental.pallas import tpu as pltpu
from jax.sharding import PartitionSpec as P

EPS = 1e-05
F32 = jnp.float32
BF16 = jnp.bfloat16
MESH = pl.DeviceIdType.MESH


def sigmoid(x):
    return 0.5 * jnp.tanh(0.5 * x) + 0.5


def mm(a, b):
    return lax.dot_general(a, b, (((1,), (0,)), ((), ())), preferred_element_type=F32)


def mm_nt(a, b):
    return lax.dot_general(a, b, (((1,), (1,)), ((), ())), preferred_element_type=F32)


def mm_tn(a, b):
    return lax.dot_general(a, b, (((0,), (0,)), ((), ())), preferred_element_type=F32)


def column(block, n, rows):
    return jnp.broadcast_to(block[0:rows, n : n + 1], (rows, 128))


def mean0(x):
    return jnp.sum(x, axis=0, keepdims=True) * (1.0 / 128.0)


def hops(n):
    return (0, 1, 2, 1)[n]


STEPS = [
    (dz, dy, dx, dc)
    for dz in range(4)
    for dy in range(4)
    for dx in range(4)
    for dc in range(2)
    if dz + dy + dx + dc
]
random.Random(4).shuffle(STEPS)
STEPS.sort(key=lambda s: -hops(s[0]) - hops(s[1]) - hops(s[2]))


def kernel(
    pair_in,
    lens,
    ln_gain_in,
    ln_bias_in,
    pw_in,
    pb_in,
    out_gain_in,
    out_bias_in,
    w_out_in,
    out_shift_in,
    w_gate_in,
    gate_bias_in,
    cot_in,
    outs,
    pair,
    cot,
    w_gate,
    wt,
    wo,
    hv,
    half,
    vec,
    pnorm,
    pscale,
    normed,
    s1f,
    s1,
    r1,
    r1f,
    lmat,
    rmat,
    s2,
    r2,
    s3f,
    s3,
    r3,
    gmat,
    s4,
    r4,
    r4f,
    factor,
    gate_t,
    cot_t,
    gs_t,
    m1_t,
    tn_t,
    part_t,
    wo_t,
    back_w,
    gp,
    wsem_s,
    wsem_r,
    ssem,
    rsem,
    isem,
):
    p = lax.axis_index("dap")
    g = lax.axis_index("ch")
    me = g * 64 + p

    z, y, x, core = p // 16, p // 4 % 4, p // 2 % 2 * 2 + g, p % 2
    turn_z, turn_y, turn_x = (
        1 + 2 * ((n + core) % 2) for n in (x + y, x + z, y + z)
    )
    at_z = [(z + n * turn_z) % 4 * 16 for n in range(4)]
    at_y = [(y + n * turn_y) % 4 * 4 for n in range(4)]
    at_x = [(x + n * turn_x) % 4 for n in range(4)]
    at_zy = [[zn + yn for yn in at_y] for zn in at_z]
    at_xc = [[xn // 2 * 2 + c for c in (core, 1 - core)] for xn in at_x]
    at_g = [xn % 2 for xn in at_x]

    def place(step):
        dz, dy, dx, dc = step
        return at_zy[dz][dy] + at_xc[dx][dc], at_g[dx]

    barrier = pltpu.get_barrier_semaphore()
    for step in STEPS:
        pl.semaphore_signal(
            barrier, inc=1, device_id=place(step), device_id_type=MESH
        )
    loads = [
        pltpu.make_async_copy(source, target, isem.at[n])
        for n, (source, target) in enumerate(
            (
                (pair_in, pair),
                (pw_in, wt.at[g]),
                (ln_gain_in, vec.at[0:1]),
                (ln_bias_in, vec.at[1:2]),
                (out_shift_in, vec.at[2:3]),
                (gate_bias_in, vec.at[3:4]),
                (pb_in, half.at[0:4]),
                (out_gain_in, half.at[4:5]),
                (out_bias_in, half.at[5:6]),
                (w_out_in, wo.at[g]),
                (w_gate_in, w_gate),
                (cot_in, cot),
            )
        )
    ]
    for load in loads:
        load.start()
    for load in loads:
        load.wait()

    hv[g] = jnp.zeros((8, 128), F32)
    hv[g, 0:6, 0:64] = half[0:6]
    vcol = vec[...].T
    gain_c = column(vcol, 0, 128)
    bias_c = column(vcol, 1, 128)
    hcol = hv[g].T
    proj_c = [column(hcol, m, 64) for m in range(4)]

    lane = lax.broadcasted_iota(jnp.int32, (1, 128), 1)
    low = lane < 64
    slot = jnp.where(low, lane, lane - 64)

    def present_columns(first_chain):
        limit = jnp.where(low, lens[first_chain], lens[first_chain + 1])
        return jnp.where(slot < limit, 1.0, 0.0)

    row_limit = jnp.full((1, 128), lens[p // 16], jnp.int32)
    row_present = [
        jnp.where(row_limit > lax.rem(p * 4 + i, 64), 1.0, 0.0) for i in range(4)
    ]

    columns = [present_columns(0), present_columns(2)]
    for i in range(4):
        for kh in range(2):
            t = i * 2 + kh
            x = pair[i, kh * 128 : (kh + 1) * 128, :].T.astype(F32)
            mean = mean0(x)
            scale = lax.rsqrt(mean0(x * x) - mean * mean + EPS)
            norm = (x - mean) * scale
            pnorm[t] = norm
            pscale[t] = scale
            nb = (norm * gain_c + bias_c).astype(BF16)
            normed[t] = nb
            mask = row_present[i] * columns[kh]
            pr = mm(wt[g], nb)
            left = sigmoid(pr[0:64] + proj_c[0]) * (pr[64:128] + proj_c[1]) * mask
            right = sigmoid(pr[128:192] + proj_c[2]) * (pr[192:256] + proj_c[3]) * mask
            s1f[pl.ds(i * 4 + kh, 64, stride=16), :] = left
            s1f[pl.ds(i * 4 + 2 + kh, 64, stride=16), :] = right
    s1[...] = s1f[...].reshape(64, 16, 128).astype(BF16)

    gate_w = w_gate[...].T
    gate_c = column(vcol, 3, 128)
    own_columns = present_columns(g * 2)
    for i in range(4):
        gate = sigmoid(mm(gate_w, normed[i * 2 + g]) + gate_c)
        gate_t[i] = gate
        cot_t[i] = cot[i].T.astype(F32)

    pl.semaphore_wait(barrier, 127)

    pltpu.make_async_copy(s1.at[p], r1.at[p], rsem.at[0]).start()
    for step in STEPS:
        if step[2] % 2 == 0:
            t, _ = place(step)
            pltpu.make_async_remote_copy(
                src_ref=s1.at[t],
                dst_ref=r1.at[p],
                send_sem=ssem.at[0],
                recv_sem=rsem.at[0],
                device_id=(t, g),
                device_id_type=MESH,
            ).start()

    swaps = [
        pltpu.make_async_remote_copy(
            src_ref=ref.at[g],
            dst_ref=ref.at[g],
            send_sem=wsem_s.at[n],
            recv_sem=wsem_r.at[n],
            device_id=(p, 1 - g),
            device_id_type=MESH,
        )
        for n, ref in enumerate((wt, wo, hv))
    ]
    for swap in swaps:
        swap.start()

    for swap in swaps:
        swap.wait()
    halves = [hv[0].T, hv[1].T]
    full = [
        jnp.concatenate([column(halves[0], n, 64), column(halves[1], n, 64)], axis=0)
        for n in (4, 5)
    ]
    wo_full = wo[...].reshape(128, 128)
    for i in range(4):
        grad_out = (cot_t[i] * gate_t[i]).astype(BF16)
        gs = mm(wo_full, grad_out) * full[0]
        gs_t[i] = gs
        m1_t[i] = mean0(gs)
    wo_t[...] = wo_full.T
    back_w[...] = wt[...].reshape(512, 128).astype(F32).T.astype(BF16)

    for h in range(2):
        bias = [column(halves[h], m, 64) for m in range(4)]
        rows = slice(h * 64, (h + 1) * 64)
        for i in range(4):
            pr = mm(wt[h], normed[i * 2 + g])
            mask = row_present[i] * own_columns
            for side in range(2):
                n = side * 2
                s = sigmoid(pr[n * 64 : n * 64 + 64] + bias[n])
                sm = s * mask
                value = pr[n * 64 + 64 : n * 64 + 128] + bias[n + 1]
                factor[i, n, rows, :] = value * sm * (1.0 - s)
                factor[i, n + 1, rows, :] = sm

    pltpu.make_async_copy(r1, r1, rsem.at[0]).wait()
    r1f[...] = r1[...].reshape(1024, 128).astype(F32)
    for kh in range(2):
        cols = slice(kh * 128, (kh + 1) * 128)
        lmat[:, cols] = r1f[pl.ds(kh, 256, stride=4), :].astype(BF16)
        rmat[:, cols] = r1f[pl.ds(2 + kh, 256, stride=4), :].astype(BF16)
    for h in range(2):
        s2[h * 256 : (h + 1) * 256, :] = mm_nt(
            lmat[...], rmat[h * 128 : (h + 1) * 128, :]
        )

    def spread(source, target, n, rows):
        def block(ref, t):
            if rows:
                return ref.at[pl.ds(pl.multiple_of(t * rows, rows), rows)]
            return ref.at[t]

        mine = block(target, me)
        pltpu.make_async_copy(block(source, me), mine, rsem.at[n]).start()
        for step in STEPS:
            t, tg = place(step)
            pltpu.make_async_remote_copy(
                src_ref=block(source, tg * 64 + t),
                dst_ref=mine,
                send_sem=ssem.at[n],
                recv_sem=rsem.at[n],
                device_id=(t, tg),
                device_id_type=MESH,
            ).start()

    spread(s2, r2, 1, 4)
    pltpu.make_async_copy(r2, r2, rsem.at[1]).wait()

    for i in range(4):
        tri = r2[pl.ds(i, 128, stride=4), :]
        mean = mean0(tri)
        scale = lax.rsqrt(mean0(tri * tri) - mean * mean + EPS)
        tn = (tri - mean) * scale
        tn_t[i] = tn
        gs = gs_t[i]
        grad = scale * (gs - m1_t[i] - tn * mean0(gs * tn))
        s3f[pl.ds(i, 128, stride=4), :] = grad
    s3[...] = s3f[...].reshape(128, 4, 128).astype(BF16)
    spread(s3, r3, 2, 0)

    shift_c = column(vcol, 2, 128)
    for i in range(4):
        tri_out = (tn_t[i] * full[0] + full[1]).astype(BF16)
        out_sum = mm(wo_t[...], tri_out) + shift_c
        gate = gate_t[i]
        gated = gate * out_sum
        outs[0, i] = gated.T.astype(BF16)
        grad_gate = (cot_t[i] * gated * (1.0 - gate)).astype(BF16)
        part_t[i] = mm(w_gate[...], grad_gate)

    pltpu.make_async_copy(r3, r3, rsem.at[2]).wait()
    for h in range(2):
        part = r3[h * 64 : (h + 1) * 64].astype(F32).reshape(256, 128)
        gmat[:, h * 128 : (h + 1) * 128] = part.astype(BF16)
    grads = (mm(gmat[...], rmat[...]), mm_tn(gmat[...], lmat[...]))
    for h in range(2):
        cols = slice(h * 128, (h + 1) * 128)
        pieces = [grad[:, cols].reshape(64, 4, 128) for grad in grads]
        s4[h * 64 : (h + 1) * 64] = jnp.concatenate(pieces, axis=1).astype(BF16)
    spread(s4, r4, 3, 0)
    pltpu.make_async_copy(r4, r4, rsem.at[3]).wait()

    r4f[...] = r4[...].astype(F32).reshape(1024, 128)
    for i in range(4):
        for side in range(2):
            edge = r4f[pl.ds(side * 4 + i, 128, stride=8), :]
            for n in range(2):
                m = side * 2 + n
                prod = (edge * factor[i, m]).astype(BF16)
                for h in range(2):
                    at = h * 256 + m * 64
                    gp[at : at + 64, i * 128 : (i + 1) * 128] = prod[
                        h * 64 : (h + 1) * 64
                    ]
    for i in range(4):
        grad = mm(back_w[...], gp[:, i * 128 : (i + 1) * 128]) + part_t[i]
        ps = grad * gain_c
        norm = pnorm[i * 2 + g]
        own = pscale[i * 2 + g] * (ps - mean0(ps) - norm * mean0(ps * norm))
        outs[1, i] = own.T.astype(BF16)

    blocks = s1.at[pl.ds(0, 63)]
    pltpu.make_async_copy(blocks, blocks, ssem.at[0]).wait()
    blocks = s2.at[pl.ds(0, 508)]
    pltpu.make_async_copy(blocks, blocks, ssem.at[1]).wait()
    for n, ref in ((2, s3), (3, s4)):
        blocks = ref.at[pl.ds(0, 127)]
        pltpu.make_async_copy(blocks, blocks, ssem.at[n]).wait()


def publish(outs, update, pair_grad, sem):
    copies = [
        pltpu.make_async_copy(outs.at[n], target, sem.at[n])
        for n, target in enumerate((update, pair_grad))
    ]
    for copy in copies:
        copy.start()
    for copy in copies:
        copy.wait()


def per_device(
    pair,
    chain_lengths,
    ln_gain,
    ln_bias,
    proj_weight,
    proj_bias,
    out_gain,
    out_bias,
    w_out,
    out_shift,
    w_gate,
    gate_bias,
    cotangent,
):
    def row(v):
        return v.reshape(1, -1)

    vmem = pl.BlockSpec(memory_space=pltpu.VMEM)
    hbm = pl.BlockSpec(memory_space=pltpu.HBM)
    smem = pl.BlockSpec(memory_space=pltpu.SMEM)
    out = jax.ShapeDtypeStruct((4, 128, 128), BF16)
    outs = pl.pallas_call(
        kernel,
        out_shape=jax.ShapeDtypeStruct((2, 4, 128, 128), BF16),
        in_specs=[hbm, smem] + [hbm] * 11,
        out_specs=vmem,
        scratch_shapes=[
            pltpu.VMEM((4, 256, 128), BF16),
            pltpu.VMEM((4, 128, 128), BF16),
            pltpu.VMEM((128, 128), BF16),
            pltpu.VMEM((2, 256, 128), BF16),
            pltpu.VMEM((2, 64, 128), BF16),
            pltpu.VMEM((2, 8, 128), F32),
            pltpu.VMEM((8, 64), F32),
            pltpu.VMEM((8, 128), F32),
            pltpu.VMEM((8, 128, 128), F32),
            pltpu.VMEM((8, 1, 128), F32),
            pltpu.VMEM((8, 128, 128), BF16),
            pltpu.VMEM((1024, 128), F32),
            pltpu.VMEM((64, 16, 128), BF16),
            pltpu.VMEM((64, 16, 128), BF16),
            pltpu.VMEM((1024, 128), F32),
            pltpu.VMEM((256, 256), BF16),
            pltpu.VMEM((256, 256), BF16),
            pltpu.VMEM((512, 128), F32),
            pltpu.VMEM((512, 128), F32),
            pltpu.VMEM((512, 128), F32),
            pltpu.VMEM((128, 4, 128), BF16),
            pltpu.VMEM((128, 4, 128), BF16),
            pltpu.VMEM((256, 256), BF16),
            pltpu.VMEM((128, 8, 128), BF16),
            pltpu.VMEM((128, 8, 128), BF16),
            pltpu.VMEM((1024, 128), F32),
            pltpu.VMEM((4, 4, 128, 128), F32),
            pltpu.VMEM((4, 128, 128), F32),
            pltpu.VMEM((4, 128, 128), F32),
            pltpu.VMEM((4, 128, 128), F32),
            pltpu.VMEM((4, 1, 128), F32),
            pltpu.VMEM((4, 128, 128), F32),
            pltpu.VMEM((4, 128, 128), F32),
            pltpu.VMEM((128, 128), BF16),
            pltpu.VMEM((128, 512), BF16),
            pltpu.VMEM((512, 512), BF16),
            pltpu.SemaphoreType.DMA((3,)),
            pltpu.SemaphoreType.DMA((3,)),
            pltpu.SemaphoreType.DMA((4,)),
            pltpu.SemaphoreType.DMA((4,)),
            pltpu.SemaphoreType.DMA((12,)),
        ],
        compiler_params=pltpu.CompilerParams(
            collective_id=0, has_side_effects=True, vmem_limit_bytes=63 << 20
        ),
    )(
        pair,
        chain_lengths,
        row(ln_gain),
        row(ln_bias),
        jnp.swapaxes(proj_weight, 1, 2).reshape(256, 128),
        proj_bias,
        row(out_gain),
        row(out_bias),
        w_out,
        row(out_shift),
        w_gate,
        row(gate_bias),
        cotangent,
    )
    return pl.pallas_call(
        publish,
        out_shape=(out, out),
        in_specs=[vmem],
        out_specs=(hbm, hbm),
        scratch_shapes=[pltpu.SemaphoreType.DMA((2,))],
    )(outs)


def solution(mesh):
    placed = (
        P("dap", None, None),
        P(),
        P(),
        P(),
        P(None, None, "ch"),
        P(None, "ch"),
        P("ch"),
        P("ch"),
        P("ch", None),
        P(),
        P(),
        P(),
        P("dap", "ch", None),
    )
    return jax.shard_map(
        per_device,
        mesh=mesh,
        in_specs=placed,
        out_specs=(P("dap", "ch", None), P("dap", "ch", None)),
        check_vma=False,
    )
```

```python
import random

import jax
import jax.numpy as jnp
from jax import lax
from jax.experimental import pallas as pl
from jax.experimental.pallas import tpu as pltpu
from jax.sharding import PartitionSpec as P

EPS = 1e-05
F32 = jnp.float32
BF16 = jnp.bfloat16
MESH = pl.DeviceIdType.MESH


def sigmoid(x):
    return 0.5 * jnp.tanh(0.5 * x) + 0.5


def mm(a, b):
    return lax.dot_general(a, b, (((1,), (0,)), ((), ())), preferred_element_type=F32)


def mm_nt(a, b):
    return lax.dot_general(a, b, (((1,), (1,)), ((), ())), preferred_element_type=F32)


def mm_tn(a, b):
    return lax.dot_general(a, b, (((0,), (0,)), ((), ())), preferred_element_type=F32)


def column(block, n, rows):
    return jnp.broadcast_to(block[0:rows, n : n + 1], (rows, 128))


def mean0(x):
    return jnp.sum(x, axis=0, keepdims=True) * (1.0 / 128.0)


def hops(n):
    return (0, 1, 2, 1)[n]


STEPS = [
    (dz, dy, dx, dc)
    for dz in range(4)
    for dy in range(4)
    for dx in range(4)
    for dc in range(2)
    if dz + dy + dx + dc
]
random.Random(1).shuffle(STEPS)
STEPS.sort(key=lambda s: -hops(s[0]) - hops(s[1]) - hops(s[2]))


def kernel(
    pair_in,
    lens,
    ln_gain_in,
    ln_bias_in,
    pw_in,
    pb_in,
    out_gain_in,
    out_bias_in,
    w_out_in,
    out_shift_in,
    w_gate_in,
    gate_bias_in,
    cot_in,
    outs,
    pair,
    cot,
    w_gate,
    wt,
    wo,
    hv,
    half,
    vec,
    pnorm,
    pscale,
    normed,
    s1f,
    s1,
    r1,
    r1f,
    lmat,
    rmat,
    s2,
    r2,
    s3f,
    s3,
    r3,
    gmat,
    s4f,
    s4,
    r4,
    r4f,
    factor,
    gate_t,
    cot_t,
    gs_t,
    m1_t,
    tn_t,
    part_t,
    wo_t,
    back_w,
    gp,
    wsem_s,
    wsem_r,
    ssem,
    rsem,
    isem,
):
    p = lax.axis_index("dap")
    g = lax.axis_index("ch")
    me = g * 64 + p

    z, y, x, core = p // 16, p // 4 % 4, p // 2 % 2 * 2 + g, p % 2
    at_z = [(z + n) % 4 * 16 for n in range(4)]
    at_y = [(y + n) % 4 * 4 for n in range(4)]
    at_x = [(x + n) % 4 for n in range(4)]
    at_zy = [[zn + yn for yn in at_y] for zn in at_z]
    at_xc = [[xn // 2 * 2 + c for c in (core, 1 - core)] for xn in at_x]
    at_g = [xn % 2 for xn in at_x]

    def place(step):
        dz, dy, dx, dc = step
        return at_zy[dz][dy] + at_xc[dx][dc], at_g[dx]

    barrier = pltpu.get_barrier_semaphore()
    for step in STEPS:
        pl.semaphore_signal(
            barrier, inc=1, device_id=place(step), device_id_type=MESH
        )
    loads = [
        pltpu.make_async_copy(source, target, isem.at[n])
        for n, (source, target) in enumerate(
            (
                (pair_in, pair),
                (pw_in, wt.at[g]),
                (ln_gain_in, vec.at[0:1]),
                (ln_bias_in, vec.at[1:2]),
                (out_shift_in, vec.at[2:3]),
                (gate_bias_in, vec.at[3:4]),
                (pb_in, half.at[0:4]),
                (out_gain_in, half.at[4:5]),
                (out_bias_in, half.at[5:6]),
                (w_out_in, wo.at[g]),
                (w_gate_in, w_gate),
                (cot_in, cot),
            )
        )
    ]
    for load in loads:
        load.start()
    for load in loads:
        load.wait()

    hv[g] = jnp.zeros((8, 128), F32)
    hv[g, 0:6, 0:64] = half[0:6]
    vcol = vec[...].T
    gain_c = column(vcol, 0, 128)
    bias_c = column(vcol, 1, 128)
    hcol = hv[g].T
    proj_c = [column(hcol, m, 64) for m in range(4)]

    lane = lax.broadcasted_iota(jnp.int32, (1, 128), 1)
    low = lane < 64
    slot = jnp.where(low, lane, lane - 64)

    def present_columns(first_chain):
        limit = jnp.where(low, lens[first_chain], lens[first_chain + 1])
        return jnp.where(slot < limit, 1.0, 0.0)

    row_limit = jnp.full((1, 128), lens[p // 16], jnp.int32)
    row_present = [
        jnp.where(row_limit > lax.rem(p * 4 + i, 64), 1.0, 0.0) for i in range(4)
    ]

    columns = [present_columns(0), present_columns(2)]
    for i in range(4):
        for kh in range(2):
            t = i * 2 + kh
            x = pair[i, kh * 128 : (kh + 1) * 128, :].T.astype(F32)
            mean = mean0(x)
            scale = lax.rsqrt(mean0(x * x) - mean * mean + EPS)
            norm = (x - mean) * scale
            pnorm[t] = norm
            pscale[t] = scale
            nb = (norm * gain_c + bias_c).astype(BF16)
            normed[t] = nb
            mask = row_present[i] * columns[kh]
            pr = mm(wt[g], nb)
            left = sigmoid(pr[0:64] + proj_c[0]) * (pr[64:128] + proj_c[1]) * mask
            right = sigmoid(pr[128:192] + proj_c[2]) * (pr[192:256] + proj_c[3]) * mask
            s1f[pl.ds(i * 4 + kh, 64, stride=16), :] = left
            s1f[pl.ds(i * 4 + 2 + kh, 64, stride=16), :] = right
    s1[...] = s1f[...].reshape(64, 16, 128).astype(BF16)

    gate_w = w_gate[...].T
    gate_c = column(vcol, 3, 128)
    own_columns = present_columns(g * 2)
    for i in range(4):
        gate = sigmoid(mm(gate_w, normed[i * 2 + g]) + gate_c)
        gate_t[i] = gate
        cot_t[i] = cot[i].T.astype(F32)

    pl.semaphore_wait(barrier, 127)

    pltpu.make_async_copy(s1.at[p], r1.at[p], rsem.at[0]).start()
    for step in STEPS:
        if step[2] % 2 == 0:
            t, _ = place(step)
            pltpu.make_async_remote_copy(
                src_ref=s1.at[t],
                dst_ref=r1.at[p],
                send_sem=ssem.at[0],
                recv_sem=rsem.at[0],
                device_id=(t, g),
                device_id_type=MESH,
            ).start()

    swaps = [
        pltpu.make_async_remote_copy(
            src_ref=ref.at[g],
            dst_ref=ref.at[g],
            send_sem=wsem_s.at[n],
            recv_sem=wsem_r.at[n],
            device_id=(p, 1 - g),
            device_id_type=MESH,
        )
        for n, ref in enumerate((wt, wo, hv))
    ]
    for swap in swaps[1:]:
        swap.start()

    for swap in swaps[1:]:
        swap.wait()
    halves = [hv[0].T, hv[1].T]
    full = [
        jnp.concatenate([column(halves[0], n, 64), column(halves[1], n, 64)], axis=0)
        for n in (4, 5)
    ]
    wo_full = wo[...].reshape(128, 128)
    for i in range(4):
        grad_out = (cot_t[i] * gate_t[i]).astype(BF16)
        gs = mm(wo_full, grad_out) * full[0]
        gs_t[i] = gs
        m1_t[i] = mean0(gs)
    wo_t[...] = wo_full.T

    pltpu.make_async_copy(r1, r1, rsem.at[0]).wait()
    r1f[...] = r1[...].reshape(1024, 128).astype(F32)
    for kh in range(2):
        cols = slice(kh * 128, (kh + 1) * 128)
        lmat[:, cols] = r1f[pl.ds(kh, 256, stride=4), :].astype(BF16)
        rmat[:, cols] = r1f[pl.ds(2 + kh, 256, stride=4), :].astype(BF16)
    for h in range(2):
        s2[h * 256 : (h + 1) * 256, :] = mm_nt(
            lmat[...], rmat[h * 128 : (h + 1) * 128, :]
        )

    def spread(source, target, n, rows):
        def block(ref, t):
            if rows:
                return ref.at[pl.ds(pl.multiple_of(t * rows, rows), rows)]
            return ref.at[t]

        mine = block(target, me)
        pltpu.make_async_copy(block(source, me), mine, rsem.at[n]).start()
        for step in STEPS:
            t, tg = place(step)
            pltpu.make_async_remote_copy(
                src_ref=block(source, tg * 64 + t),
                dst_ref=mine,
                send_sem=ssem.at[n],
                recv_sem=rsem.at[n],
                device_id=(t, tg),
                device_id_type=MESH,
            ).start()

    spread(s2, r2, 1, 4)
    pltpu.make_async_copy(r2, r2, rsem.at[1]).wait()

    for i in range(4):
        tri = r2[pl.ds(i, 128, stride=4), :]
        mean = mean0(tri)
        scale = lax.rsqrt(mean0(tri * tri) - mean * mean + EPS)
        tn = (tri - mean) * scale
        tn_t[i] = tn
        gs = gs_t[i]
        grad = scale * (gs - m1_t[i] - tn * mean0(gs * tn))
        s3f[pl.ds(i, 128, stride=4), :] = grad
    s3[...] = s3f[...].reshape(128, 4, 128).astype(BF16)
    spread(s3, r3, 2, 0)
    swaps[0].start()

    shift_c = column(vcol, 2, 128)
    for i in range(4):
        tri_out = (tn_t[i] * full[0] + full[1]).astype(BF16)
        out_sum = mm(wo_t[...], tri_out) + shift_c
        gate = gate_t[i]
        gated = gate * out_sum
        outs[0, i] = gated.T.astype(BF16)
        grad_gate = (cot_t[i] * gated * (1.0 - gate)).astype(BF16)
        part_t[i] = mm(w_gate[...], grad_gate)

    pltpu.make_async_copy(r3, r3, rsem.at[2]).wait()
    for h in range(2):
        part = r3[h * 64 : (h + 1) * 64].astype(F32).reshape(256, 128)
        gmat[:, h * 128 : (h + 1) * 128] = part.astype(BF16)
    grads = (mm(gmat[...], rmat[...]), mm_tn(gmat[...], lmat[...]))
    for side in range(2):
        for h in range(2):
            s4f[pl.ds(h * 512 + side, 256, stride=2), :] = grads[side][
                :, h * 128 : (h + 1) * 128
            ]
    s4[...] = s4f[...].reshape(128, 8, 128).astype(BF16)
    spread(s4, r4, 3, 0)

    swaps[0].wait()
    back_w[...] = wt[...].reshape(512, 128).astype(F32).T.astype(BF16)

    for h in range(2):
        bias = [column(halves[h], m, 64) for m in range(4)]
        rows = slice(h * 64, (h + 1) * 64)
        for i in range(4):
            pr = mm(wt[h], normed[i * 2 + g])
            mask = row_present[i] * own_columns
            for side in range(2):
                n = side * 2
                s = sigmoid(pr[n * 64 : n * 64 + 64] + bias[n])
                sm = s * mask
                value = pr[n * 64 + 64 : n * 64 + 128] + bias[n + 1]
                factor[i, n, rows, :] = value * sm * (1.0 - s)
                factor[i, n + 1, rows, :] = sm

    pltpu.make_async_copy(r4, r4, rsem.at[3]).wait()

    r4f[...] = r4[...].astype(F32).reshape(1024, 128)
    for i in range(4):
        for side in range(2):
            edge = r4f[pl.ds(i * 2 + side, 128, stride=8), :]
            for n in range(2):
                m = side * 2 + n
                prod = (edge * factor[i, m]).astype(BF16)
                for h in range(2):
                    at = h * 256 + m * 64
                    gp[at : at + 64, i * 128 : (i + 1) * 128] = prod[
                        h * 64 : (h + 1) * 64
                    ]
    for i in range(4):
        grad = mm(back_w[...], gp[:, i * 128 : (i + 1) * 128]) + part_t[i]
        ps = grad * gain_c
        norm = pnorm[i * 2 + g]
        own = pscale[i * 2 + g] * (ps - mean0(ps) - norm * mean0(ps * norm))
        outs[1, i] = own.T.astype(BF16)

    blocks = s1.at[pl.ds(0, 63)]
    pltpu.make_async_copy(blocks, blocks, ssem.at[0]).wait()
    blocks = s2.at[pl.ds(0, 508)]
    pltpu.make_async_copy(blocks, blocks, ssem.at[1]).wait()
    for n, ref in ((2, s3), (3, s4)):
        blocks = ref.at[pl.ds(0, 127)]
        pltpu.make_async_copy(blocks, blocks, ssem.at[n]).wait()


def publish(outs, update, pair_grad, sem):
    copies = [
        pltpu.make_async_copy(outs.at[n], target, sem.at[n])
        for n, target in enumerate((update, pair_grad))
    ]
    for copy in copies:
        copy.start()
    for copy in copies:
        copy.wait()


def per_device(
    pair,
    chain_lengths,
    ln_gain,
    ln_bias,
    proj_weight,
    proj_bias,
    out_gain,
    out_bias,
    w_out,
    out_shift,
    w_gate,
    gate_bias,
    cotangent,
):
    def row(v):
        return v.reshape(1, -1)

    vmem = pl.BlockSpec(memory_space=pltpu.VMEM)
    hbm = pl.BlockSpec(memory_space=pltpu.HBM)
    smem = pl.BlockSpec(memory_space=pltpu.SMEM)
    out = jax.ShapeDtypeStruct((4, 128, 128), BF16)
    outs = pl.pallas_call(
        kernel,
        out_shape=jax.ShapeDtypeStruct((2, 4, 128, 128), BF16),
        in_specs=[hbm, smem] + [hbm] * 11,
        out_specs=vmem,
        scratch_shapes=[
            pltpu.VMEM((4, 256, 128), BF16),
            pltpu.VMEM((4, 128, 128), BF16),
            pltpu.VMEM((128, 128), BF16),
            pltpu.VMEM((2, 256, 128), BF16),
            pltpu.VMEM((2, 64, 128), BF16),
            pltpu.VMEM((2, 8, 128), F32),
            pltpu.VMEM((8, 64), F32),
            pltpu.VMEM((8, 128), F32),
            pltpu.VMEM((8, 128, 128), F32),
            pltpu.VMEM((8, 1, 128), F32),
            pltpu.VMEM((8, 128, 128), BF16),
            pltpu.VMEM((1024, 128), F32),
            pltpu.VMEM((64, 16, 128), BF16),
            pltpu.VMEM((64, 16, 128), BF16),
            pltpu.VMEM((1024, 128), F32),
            pltpu.VMEM((256, 256), BF16),
            pltpu.VMEM((256, 256), BF16),
            pltpu.VMEM((512, 128), F32),
            pltpu.VMEM((512, 128), F32),
            pltpu.VMEM((512, 128), F32),
            pltpu.VMEM((128, 4, 128), BF16),
            pltpu.VMEM((128, 4, 128), BF16),
            pltpu.VMEM((256, 256), BF16),
            pltpu.VMEM((1024, 128), F32),
            pltpu.VMEM((128, 8, 128), BF16),
            pltpu.VMEM((128, 8, 128), BF16),
            pltpu.VMEM((1024, 128), F32),
            pltpu.VMEM((4, 4, 128, 128), F32),
            pltpu.VMEM((4, 128, 128), F32),
            pltpu.VMEM((4, 128, 128), F32),
            pltpu.VMEM((4, 128, 128), F32),
            pltpu.VMEM((4, 1, 128), F32),
            pltpu.VMEM((4, 128, 128), F32),
            pltpu.VMEM((4, 128, 128), F32),
            pltpu.VMEM((128, 128), BF16),
            pltpu.VMEM((128, 512), BF16),
            pltpu.VMEM((512, 512), BF16),
            pltpu.SemaphoreType.DMA((3,)),
            pltpu.SemaphoreType.DMA((3,)),
            pltpu.SemaphoreType.DMA((4,)),
            pltpu.SemaphoreType.DMA((4,)),
            pltpu.SemaphoreType.DMA((12,)),
        ],
        compiler_params=pltpu.CompilerParams(
            collective_id=0, has_side_effects=True, vmem_limit_bytes=63 << 20
        ),
    )(
        pair,
        chain_lengths,
        row(ln_gain),
        row(ln_bias),
        jnp.swapaxes(proj_weight, 1, 2).reshape(256, 128),
        proj_bias,
        row(out_gain),
        row(out_bias),
        w_out,
        row(out_shift),
        w_gate,
        row(gate_bias),
        cotangent,
    )
    return pl.pallas_call(
        publish,
        out_shape=(out, out),
        in_specs=[vmem],
        out_specs=(hbm, hbm),
        scratch_shapes=[pltpu.SemaphoreType.DMA((2,))],
    )(outs)


def solution(mesh):
    placed = (
        P("dap", None, None),
        P(),
        P(),
        P(),
        P(None, None, "ch"),
        P(None, "ch"),
        P("ch"),
        P("ch"),
        P("ch", None),
        P(),
        P(),
        P(),
        P("dap", "ch", None),
    )
    return jax.shard_map(
        per_device,
        mesh=mesh,
        in_specs=placed,
        out_specs=(P("dap", "ch", None), P("dap", "ch", None)),
        check_vma=False,
    )
```
